32 devices in a mesh: seq: 8 (over z, core), tp: 4 (over y, x).
Axes of the slice: x: 2, y: 2, z: 4, core: 2. Of those that a mesh axis runs over, the one named last changes fastest.
Arguments:
- block_input: bfloat16 [8192, 2048], P('seq'), may hold values from -6 to 6
- norm_one: float32 [2048], replicated, may hold values from 0.1 to 1.9
- w_query: bfloat16 [2048, 2048], P(None, 'tp'), may hold values from -0.1875 to 0.1875
- w_key: bfloat16 [2048, 2048], P(None, 'tp'), may hold values from -0.1875 to 0.1875
- w_value: bfloat16 [2048, 2048], P(None, 'tp'), may hold values from -0.125 to 0.125
- w_out: bfloat16 [2048, 2048], P('tp'), may hold values from -0.75 to 0.75
- norm_two: float32 [2048], replicated, may hold values from 0.1 to 1.9
- w_gate: bfloat16 [2048, 5504], P(None, 'tp'), may hold values from -0.125 to 0.125
- w_up: bfloat16 [2048, 5504], P(None, 'tp'), may hold values from -0.125 to 0.125
- w_down: bfloat16 [5504, 2048], P('tp'), may hold values from -0.078125 to 0.078125
- starts: int32 [8192], P('seq'), may hold values from 0 to 8191, as said below
- cotangent: bfloat16 [8192, 2048], P('seq'), may hold values from -6 to 6
Outputs:
- output: bfloat16 [8192, 2048], P('seq')
- grad_input: float32 [8192, 2048], P('seq')
- grad_norm_one: float32 [2048], P('seq')
- grad_query: float32 [2048, 2048], P('seq', 'tp')
- grad_key: float32 [2048, 2048], P('seq', 'tp')
- grad_value: float32 [2048, 2048], P('seq', 'tp')
- grad_out: float32 [2048, 2048], P('tp', 'seq')
- grad_norm_two: float32 [2048], P('seq')
- grad_gate: float32 [2048, 5504], P('seq', 'tp')
- grad_up: float32 [2048, 5504], P('seq', 'tp')
- grad_down: float32 [5504, 2048], P('tp', 'seq')
The draws below stay inside these ranges and needn't reach their ends.
Inputs may be any that keep to these rules, and one draw needn't show every extreme that they name: starts never falls along the tokens, starts[i] <= i, and all tokens from starts[i] to i have the same start: at most five sequences laid end to end. One of them begins within the first 1024 tokens and ends within the last 1024.
All inputs are finite; a program needn't handle non-finite values.
Results may differ from the reference program's by a relative error of at most 0.015.
The reference program's roundings to bfloat16 on the way count: a program that leaves them out, or rounds other values in their place, can miss the bound.
Values may be sent and summed in bfloat16 or wider, within the bound.
No kernel may reach another device: no remote copies, remote signals or barrier semaphores. Data moves between devices by JAX's collectives and lax.ppermute only.
A program may use at most 320 MiB of HBM per device.

```python
import jax
import jax.numpy as jnp
from jax import lax

D = 2048
HEADS = 16
HEAD = 128
FF = 5504
WINDOW = 2048
TOK_DEV = 1024
TOKENS = 8192


def draw_starts(key, part):
    key = jax.random.fold_in(key, 17)
    key_a, key_b, key_c, key_d = jax.random.split(key, 4)
    first_end = jax.random.randint(key_a, (), 1, TOK_DEV)
    first_cut = jax.random.randint(key_b, (), 0, first_end)
    last_begin = TOKENS - jax.random.randint(key_c, (), 1, TOK_DEV)
    last_cut = jax.random.randint(key_d, (), last_begin, TOKENS)
    cuts = jnp.stack([jnp.zeros((), jnp.int32), first_cut, first_end, last_begin, last_cut]).astype(jnp.int32)
    positions = jnp.arange(TOKENS, dtype=jnp.int32)
    chosen = jnp.where(cuts[None, :] <= positions[:, None], cuts[None, :], 0)
    return jnp.max(chosen, axis=1).astype(jnp.int32)


def raised(values, rng, source, target, blocks, factor):
    owner, partner = [(jnp.arange(values.shape[axis_at]) // (values.shape[axis_at] // blocks)).reshape([-1 if axis == axis_at else 1 for axis in range(values.ndim)]) for axis_at in (source, target)]
    chosen = jax.random.permutation(rng, blocks)[partner]
    strong = (owner == chosen) | (owner == (partner + blocks // 2) % blocks)
    return jnp.where(strong, factor * values, values)


def block_levels(stream_key, dims, cuts, least, largest):
    level = 1.0
    for axis_at, blocks in cuts:
        heights = jax.random.uniform(jax.random.fold_in(jax.random.fold_in(stream_key, 6), axis_at), (blocks,), jnp.float32, least / len(cuts), largest / len(cuts))
        level = level * jnp.repeat(jnp.exp(heights), dims[axis_at] // blocks).reshape((-1,) + (1,) * (len(dims) - 1 - axis_at))
    return level


def noise(key, dims, scale, bound, pieces=(), kind=jnp.bfloat16):
    entries = jax.random.normal(key, dims, jnp.float32) * scale
    if len(pieces) > 0:
        entries = block_levels(key, dims, pieces, -0.22, 0.18) * entries
    return jnp.clip(entries, min=-bound, max=bound).astype(kind)


def noise_with(rng, shape, width, limit, shards, heavy, held_as=jnp.bfloat16):
    drawn = width * jax.random.normal(rng, shape, jnp.float32)
    if shards:
        drawn = drawn * block_levels(rng, shape, shards, -0.22, 0.18)
    return jnp.clip(raised(drawn, jax.random.fold_in(rng, 3), *heavy), -limit, limit).astype(held_as)


def setup_inputs(seed: int = 0) -> dict:
    streams_of = jax.random.split(jax.random.key(seed), 13)
    block_input = noise(streams_of[0], (TOKENS, D), 1.0, 6.0, ((0, 8),))
    norm_one = jnp.clip(1.0 + 0.18 * jax.random.normal(streams_of[1], (D,), jnp.float32), 0.1, 1.9)
    w_query = noise(streams_of[2], (D, D), (D // 2) ** -0.5, 0.1875, ((1, 4),))
    w_key = noise(streams_of[3], (D, D), (D // 2) ** -0.5, 0.1875, ((1, 4),))
    w_value = noise(streams_of[4], (D, D), D ** -0.5, 0.125, ((1, 4),))
    w_out = noise(streams_of[5], (D, D), (D // 32) ** -0.5, 0.75, ((0, 4),))
    norm_two = jnp.clip(1.0 + 0.18 * jax.random.normal(streams_of[6], (D,), jnp.float32), 0.1, 1.9)
    w_gate = noise(streams_of[7], (D, FF), D ** -0.5, 0.125, ((1, 4),))
    w_up = noise(streams_of[8], (D, FF), D ** -0.5, 0.125, ((1, 4),))
    w_down = noise(streams_of[9], (FF, D), FF ** -0.5, 0.078125, ((0, 4),))
    starts = draw_starts(jax.random.fold_in(streams_of[12], 71), 0)
    cotangent = noise_with(streams_of[11], (TOKENS, D), 1.0, 6.0, ((0, 8),), (0, 1, 8, 2.0))
    return {"block_input": block_input, "norm_one": norm_one, "w_query": w_query, "w_key": w_key, "w_value": w_value, "w_out": w_out, "norm_two": norm_two, "w_gate": w_gate, "w_up": w_up, "w_down": w_down, "starts": starts, "cotangent": cotangent}


@jax.custom_vjp
def low(v):
    return lax.optimization_barrier(v.astype(jnp.bfloat16)).astype(jnp.float32)

@jax.custom_vjp
def low_back(v):
    return v

def low_keep(v):
    return (low(v), None)

def low_pass(kept, grad):
    return (grad,)

def back_keep(v):
    return (v, None)

def back_low(kept, grad):
    return (low(grad),)
low.defvjp(low_keep, low_pass)
low_back.defvjp(back_keep, back_low)

def normalize(values, gain):
    factor = lax.rsqrt(lax.optimization_barrier(jnp.mean(values * values, axis=-1, keepdims=True)) + 1e-06)
    return values * factor * gain

def rotary_tables(positions):
    half_head = HEAD // 2
    freqs = 10000.0 ** (-2.0 * jnp.arange(half_head, dtype=jnp.float32) / HEAD)
    angles = positions.astype(jnp.float32)[:, None] * freqs[None, :]
    return (jnp.cos(angles), jnp.sin(angles))

def rotate(values, cosine, sine_table):
    half_head = values.shape[-1] // 2
    lower_half = values[..., :half_head]
    upper_half = values[..., half_head:]
    cos_wide = cosine[:, None, :]
    sin_wide = sine_table[:, None, :]
    return jnp.concatenate([lower_half * cos_wide - upper_half * sin_wide, upper_half * cos_wide + lower_half * sin_wide], axis=-1)

def attend(query, key_rot, value, starts):
    highest = lax.Precision.HIGHEST
    tokens = query.shape[0]
    blocks = tokens // TOK_DEV
    padding = jnp.zeros((WINDOW, HEADS, HEAD), jnp.float32)
    key_pad = jnp.concatenate([padding, key_rot], axis=0)
    value_pad = jnp.concatenate([padding, value], axis=0)
    scale = HEAD ** (-0.5)

    def one_block(block):
        begin = (block * TOK_DEV).astype(jnp.int32)
        query_blk = lax.dynamic_slice_in_dim(query, begin, TOK_DEV, 0)
        key_blk = lax.dynamic_slice_in_dim(key_pad, begin, WINDOW + TOK_DEV, 0)
        value_blk = lax.dynamic_slice_in_dim(value_pad, begin, WINDOW + TOK_DEV, 0)
        start_blk = lax.dynamic_slice_in_dim(starts, begin, TOK_DEV, 0)
        row_index = begin + jnp.arange(TOK_DEV, dtype=jnp.int32)
        col_index = begin - WINDOW + jnp.arange(WINDOW + TOK_DEV, dtype=jnp.int32)
        allowed = (col_index[None, :] <= row_index[:, None]) & (col_index[None, :] > row_index[:, None] - WINDOW) & (col_index[None, :] >= start_blk[:, None])
        scores = jnp.einsum('qhd,khd->hqk', query_blk, key_blk, precision=highest) * scale
        scores = low_back(scores)
        scores = jnp.where(allowed[None], scores, -1e+30)
        peak = lax.optimization_barrier(jnp.max(scores, axis=-1, keepdims=True))
        expo = jnp.exp(scores - peak)
        probs = low(expo / lax.optimization_barrier(jnp.sum(expo, axis=-1, keepdims=True)))
        result = jnp.einsum('hqk,khd->qhd', probs, value_blk, precision=highest)
        return result.reshape(TOK_DEV, HEADS * HEAD)
    outputs = lax.map(jax.checkpoint(one_block), jnp.arange(blocks, dtype=jnp.int32))
    return outputs.reshape(tokens, HEADS * HEAD)

def forward(block_input, norm_one, w_query, w_key, w_value, w_out, norm_two, w_gate, w_up, w_down, starts):
    highest = lax.Precision.HIGHEST
    tokens = block_input.shape[0]
    positions = jnp.arange(tokens, dtype=jnp.int32) - starts
    cosine, sine_table = rotary_tables(positions)
    hidden_one = low(normalize(block_input, norm_one))
    query_pre = low_back(jnp.dot(hidden_one, w_query, precision=highest)).reshape(tokens, HEADS, HEAD)
    key_pre = low_back(jnp.dot(hidden_one, w_key, precision=highest)).reshape(tokens, HEADS, HEAD)
    value = low(low_back(jnp.dot(hidden_one, w_value, precision=highest))).reshape(tokens, HEADS, HEAD)
    query = low(rotate(query_pre, cosine, sine_table))
    key_rot = low(rotate(key_pre, cosine, sine_table))
    attended = low(low_back(attend(query, key_rot, value, starts)))
    mid = block_input + low_back(jnp.dot(attended, w_out, precision=highest))
    hidden_two = low(normalize(mid, norm_two))
    gate = low_back(jnp.dot(hidden_two, w_gate, precision=highest))
    up_proj = low_back(jnp.dot(hidden_two, w_up, precision=highest))
    activation = low(jax.nn.silu(gate) * up_proj)
    return mid + jnp.dot(activation, w_down, precision=highest)

def reference(block_input, norm_one, w_query, w_key, w_value, w_out, norm_two, w_gate, w_up, w_down, starts, cotangent):
    floats = tuple((item.astype(jnp.float32) for item in (block_input, norm_one, w_query, w_key, w_value, w_out, norm_two, w_gate, w_up, w_down)))

    def apply_block(*params):
        return forward(*params, starts)
    result, pull = jax.vjp(apply_block, *floats)
    grads = pull(cotangent.astype(jnp.float32))
    return (result.astype(jnp.bfloat16), grads[0], grads[1], grads[2], grads[3], grads[4], grads[5], grads[6], grads[7], grads[8], grads[9])
```

```python
import jax
import jax.numpy as jnp
from jax import lax
from jax.experimental import pallas as pl
from jax.experimental.pallas import tpu as pltpu
from jax.sharding import PartitionSpec as P

HEAD = 128
WINDOW = 2048
LOG2E = 1.4426950408889634
SCALE = HEAD ** (-0.5)
NEG = -1e30
F32 = jnp.float32
BF16 = jnp.bfloat16
MIB = 1024 * 1024

NN = (((1,), (0,)), ((), ()))
NT = (((1,), (1,)), ((), ()))
TN = (((0,), (0,)), ((), ()))


def mm(a, b, dims=NN):
    return lax.dot_general(a, b, dims, preferred_element_type=F32)


def to_relative(array, me, n):
    rows = array.shape[0] // n
    return jnp.concatenate(
        [lax.dynamic_slice_in_dim(array, (r ^ me) * rows, rows, 0) for r in range(n)], axis=0
    )


def to_natural(blocks, me):
    rows = blocks[0].shape[0]
    whole = jnp.zeros((rows * len(blocks),) + blocks[0].shape[1:], blocks[0].dtype)
    for r, block in enumerate(blocks):
        whole = lax.dynamic_update_slice_in_dim(whole, block, (r ^ me) * rows, 0)
    return whole


def swap(array, bit, axis="tp"):
    size = lax.axis_size(axis)
    return lax.ppermute(array, axis, [(i, i ^ bit) for i in range(size)])


def bits_of(n):
    return [1 << b for b in range(n.bit_length() - 1)]


def sum_blocks(part, n):
    rows, width = part.shape[0] // n, part.shape[1]
    halves = []
    for half, order in enumerate((bits_of(n), bits_of(n)[::-1])):
        columns = slice(half * width // 2, (half + 1) * width // 2)
        held = {r: part[r * rows : (r + 1) * rows, columns] for r in range(n)}
        for bit in order:
            sent = [r for r in held if r & bit]
            got = swap(jnp.concatenate([held[r] for r in sent]).astype(BF16), bit)
            held = {
                r ^ bit: held[r ^ bit].astype(F32)
                + got[k * rows : (k + 1) * rows].astype(F32)
                for k, r in enumerate(sent)
            }
        halves.append(held[0])
    return jnp.concatenate(halves, axis=1)


def all_blocks(own, n):
    rows, width = own.shape
    halves = []
    for half, order in enumerate((bits_of(n)[::-1], bits_of(n))):
        held = {0: own[:, half * width // 2 : (half + 1) * width // 2]}
        for bit in order:
            have = sorted(held)
            got = swap(jnp.concatenate([held[r] for r in have]), bit)
            for k, r in enumerate(have):
                held[r ^ bit] = got[k * rows : (k + 1) * rows]
        halves.append(held)
    return [jnp.concatenate([half[r] for half in halves], axis=1) for r in range(n)]


def rotated(a, cosine, sine):
    return a * cosine + pltpu.roll(a, HEAD // 2, 1) * sine


def qkv_kernel(me_ref, x_ref, gain_ref, wq_ref, wk_ref, wv_ref, cos_ref, sin_ref, h_ref, q_ref, k_ref, v_ref):
    x = x_ref[...].astype(F32)
    factor = lax.rsqrt(jnp.mean(x * x, axis=-1, keepdims=True) + 1e-06)
    hidden = (x * factor * gain_ref[...]).astype(BF16)
    h_ref[...] = hidden
    cosine, sine = cos_ref[...], sin_ref[...]
    for w_ref, out_ref in ((wk_ref, k_ref), (wq_ref, q_ref)):
        pre = mm(hidden, w_ref[...])
        for head in range(pre.shape[1] // HEAD):
            cols = slice(head * HEAD, (head + 1) * HEAD)
            out_ref[:, cols] = rotated(pre[:, cols], cosine, sine).astype(BF16)
    v_ref[...] = mm(hidden, wv_ref[...]).astype(BF16)


def qkv(me, x, gain, wq, wk, wv, cosine, sine, n):
    tokens, width = x.shape
    local = wq.shape[1]
    rows = tokens // n
    whole = lambda r, m: (0, 0)
    mine = lambda r, m: (r, 0)
    return pl.pallas_call(
        qkv_kernel,
        grid_spec=pltpu.PrefetchScalarGridSpec(
            num_scalar_prefetch=1,
            grid=(n,),
            in_specs=[
                pl.BlockSpec((rows, width), lambda r, m: (r ^ m[0], 0)),
                pl.BlockSpec((1, width), whole),
                pl.BlockSpec((width, local), whole),
                pl.BlockSpec((width, local), whole),
                pl.BlockSpec((width, local), whole),
                pl.BlockSpec((rows, HEAD), mine),
                pl.BlockSpec((rows, HEAD), mine),
            ],
            out_specs=[
                pl.BlockSpec((rows, width), mine),
                pl.BlockSpec((rows, local), mine),
                pl.BlockSpec((rows, local), mine),
                pl.BlockSpec((rows, local), mine),
            ],
        ),
        out_shape=[
            jax.ShapeDtypeStruct((tokens, width), BF16),
            jax.ShapeDtypeStruct((tokens, local), BF16),
            jax.ShapeDtypeStruct((tokens, local), BF16),
            jax.ShapeDtypeStruct((tokens, local), BF16),
        ],
        compiler_params=pltpu.CompilerParams(vmem_limit_bytes=40 * MIB),
        cost_estimate=pl.CostEstimate(
            flops=6 * tokens * width * local,
            bytes_accessed=4 * tokens * width + 6 * (tokens + width) * local,
            transcendentals=0,
        ),
        name="project",
    )(me, x, gain, wq, wk, wv, cosine, sine)


def key_rows(me, rb, c, n, rows):
    w = rb + c
    stored = ((w & ~(n - 1)) | ((w & (n - 1)) ^ me)) * rows
    return pl.multiple_of(stored, rows), w * rows


def masked(s, first, low, query_at, diagonal):
    key_at = first + lax.broadcasted_iota(jnp.int32, s.shape, 0)
    keep = key_at >= low
    if diagonal:
        keep = keep & (key_at <= query_at)
    return jnp.where(keep, s, NEG)


def attend_kernel(n, me_ref, q_ref, k_ref, v_ref, low_ref, o_ref, lse_ref, s_ref, vt_ref):
    rows = q_ref.shape[0]
    me = me_ref[0]
    r = pl.program_id(1)
    rb = r ^ me
    chunks = 2 * n + 1

    @pl.when(r == 0)
    def _():
        for c in range(3 * n):
            cut = slice(c * rows, (c + 1) * rows)
            vt_ref[:, cut] = v_ref[cut, :].T

    q = q_ref[...]
    low = low_ref[...]
    query_at = (rb + 2 * n) * rows + lax.broadcasted_iota(jnp.int32, (1, rows), 1)
    top = jnp.full((1, rows), NEG, F32)
    for c in range(chunks):
        stored, first = key_rows(me, rb, c, n, rows)
        s = mm(k_ref[pl.ds(stored, rows), :], q, NT)
        s = masked(s, first, low, query_at, c == chunks - 1)
        s_ref[c * rows : (c + 1) * rows, :] = s
        top = jnp.maximum(top, jnp.max(s, axis=0, keepdims=True))
    top = top * (SCALE * LOG2E)
    total = jnp.zeros((1, rows), F32)
    acc = jnp.zeros((HEAD, rows), F32)
    for c in range(chunks):
        stored, first = key_rows(me, rb, c, n, rows)
        p = jnp.exp2(s_ref[c * rows : (c + 1) * rows, :] * (SCALE * LOG2E) - top)
        total = total + jnp.sum(p, axis=0, keepdims=True)
        acc = acc + mm(vt_ref[:, pl.ds(stored, rows)], p.astype(BF16))
    o_ref[...] = (acc / total).T.astype(BF16)
    lse_ref[...] = (top + jnp.log2(total)).reshape(lse_ref.shape)


def attend(me, q, keys, values, low, n):
    tokens, local = q.shape
    heads = local // HEAD
    rows = tokens // n
    window = keys.shape[0]
    pairs = heads * tokens * (2 * tokens + rows)
    return pl.pallas_call(
        lambda *refs: attend_kernel(n, *refs),
        grid_spec=pltpu.PrefetchScalarGridSpec(
            num_scalar_prefetch=1,
            grid=(heads, n),
            in_specs=[
                pl.BlockSpec((rows, HEAD), lambda h, r, m: (r, h)),
                pl.BlockSpec((window, HEAD), lambda h, r, m: (0, h)),
                pl.BlockSpec((window, HEAD), lambda h, r, m: (0, h)),
                pl.BlockSpec((1, rows), lambda h, r, m: (0, r)),
            ],
            out_specs=[
                pl.BlockSpec((rows, HEAD), lambda h, r, m: (r, h)),
                pl.BlockSpec((1, 1, rows), lambda h, r, m: (h, 0, r)),
            ],
            scratch_shapes=[
                pltpu.VMEM(((2 * n + 1) * rows, rows), F32),
                pltpu.VMEM((HEAD, window), BF16),
            ],
        ),
        out_shape=[
            jax.ShapeDtypeStruct((tokens, local), BF16),
            jax.ShapeDtypeStruct((heads, 1, tokens), F32),
        ],
        compiler_params=pltpu.CompilerParams(vmem_limit_bytes=40 * MIB),
        cost_estimate=pl.CostEstimate(
            flops=8 * pairs * HEAD, bytes_accessed=16 * tokens * local, transcendentals=pairs
        ),
        name="attend",
    )(me, q, keys, values, low)


def attend_back_kernel(
    n, me_ref, q_ref, k_ref, v_ref, low_ref, o_ref, do_ref, lse_ref, cos_ref, sin_ref,
    dq_ref, dk_ref, dv_ref, dk_acc, dv_acc, kt_ref,
):
    rows = q_ref.shape[0]
    me = me_ref[0]
    r = pl.program_id(1)
    rb = r ^ me
    chunks = 2 * n + 1

    @pl.when(r == 0)
    def _():
        for c in range(3 * n):
            cut = slice(c * rows, (c + 1) * rows)
            kt_ref[:, cut] = k_ref[cut, :].T
            dk_acc[cut, :] = jnp.zeros((rows, HEAD), F32)
            dv_acc[cut, :] = jnp.zeros((rows, HEAD), F32)

    q, do = q_ref[...], do_ref[...]
    low = low_ref[...]
    lse = lse_ref[...].reshape(1, rows)
    delta = jnp.sum((do.astype(F32) * o_ref[...].astype(F32)).T, axis=0, keepdims=True)
    query_at = (rb + 2 * n) * rows + lax.broadcasted_iota(jnp.int32, (1, rows), 1)
    dqt = jnp.zeros((HEAD, rows), F32)
    for c in range(chunks):
        stored, first = key_rows(me, rb, c, n, rows)
        here = pl.ds(stored, rows)
        s = mm(k_ref[here, :], q, NT) * (SCALE * LOG2E)
        s = masked(s, first, low, query_at, c == chunks - 1)
        p = jnp.exp2(s - lse)
        dv_acc[here, :] += mm(p.astype(BF16), do)
        dp = mm(v_ref[here, :], do, NT)
        ds = (p * (dp - delta)).astype(BF16)
        dk_acc[here, :] += mm(ds, q)
        dqt = dqt + mm(kt_ref[:, here], ds)
    dq_ref[...] = rotated(dqt.T * SCALE, cos_ref[...], -sin_ref[...]).astype(BF16)

    @pl.when(r == n - 1)
    def _():
        for c in range(3 * n):
            cut = slice(c * rows, (c + 1) * rows)
            dk_ref[cut, :] = (dk_acc[cut, :] * SCALE).astype(BF16)
            dv_ref[cut, :] = dv_acc[cut, :].astype(BF16)


def attend_back(me, q, keys, values, low, attended, d_attended, lse, cosine, sine, n):
    tokens, local = q.shape
    heads = local // HEAD
    rows = tokens // n
    window = keys.shape[0]
    pairs = heads * tokens * (2 * tokens + rows)
    block = pl.BlockSpec((rows, HEAD), lambda h, r, m: (r, h))
    whole = pl.BlockSpec((window, HEAD), lambda h, r, m: (0, h))
    table = pl.BlockSpec((rows, HEAD), lambda h, r, m: (r, 0))
    return pl.pallas_call(
        lambda *refs: attend_back_kernel(n, *refs),
        grid_spec=pltpu.PrefetchScalarGridSpec(
            num_scalar_prefetch=1,
            grid=(heads, n),
            in_specs=[
                block,
                whole,
                whole,
                pl.BlockSpec((1, rows), lambda h, r, m: (0, r)),
                block,
                block,
                pl.BlockSpec((1, 1, rows), lambda h, r, m: (h, 0, r)),
                table,
                table,
            ],
            out_specs=[block, whole, whole],
            scratch_shapes=[
                pltpu.VMEM((window, HEAD), F32),
                pltpu.VMEM((window, HEAD), F32),
                pltpu.VMEM((HEAD, window), BF16),
            ],
        ),
        out_shape=[
            jax.ShapeDtypeStruct((tokens, local), BF16),
            jax.ShapeDtypeStruct((window, local), BF16),
            jax.ShapeDtypeStruct((window, local), BF16),
        ],
        compiler_params=pltpu.CompilerParams(vmem_limit_bytes=40 * MIB),
        cost_estimate=pl.CostEstimate(
            flops=20 * pairs * HEAD, bytes_accessed=30 * tokens * local, transcendentals=pairs
        ),
        name="attend_back",
    )(me, q, keys, values, low, attended, d_attended, lse, cosine, sine)


def rotate_wide(values, cosine, sine):
    tokens, local = values.shape
    split = values.reshape(tokens, local // HEAD, 2, HEAD // 2)
    swapped = jnp.concatenate([split[:, :, 1:], split[:, :, :1]], axis=2).reshape(tokens, local)
    heads = local // HEAD
    return values * jnp.tile(cosine, (1, heads)) + swapped * jnp.tile(sine, (1, heads))


def gain_sums(sums, n):
    for bit in bits_of(n):
        sums = sums + swap(sums, bit)
    peers = lax.axis_size("seq")
    at = lax.axis_index("seq")
    for bit in bits_of(peers)[::-1]:
        half = sums.shape[1] // 2
        upper = (at & bit) != 0
        low_part, high_part = sums[:, :half], sums[:, half:]
        kept = jnp.where(upper, high_part, low_part)
        sums = kept + swap(jnp.where(upper, low_part, high_part), bit, "seq")
    return sums


def scattered(grad, dim):
    return lax.psum_scatter(grad.astype(BF16), "seq", scatter_dimension=dim, tiled=True).astype(F32)


def on_device(
    block_input, norm_one, w_query, w_key, w_value, w_out, norm_two, w_gate, w_up, w_down,
    starts, cotangent,
):
    tokens, width = block_input.shape
    n = lax.axis_size("tp")
    me = lax.axis_index("tp")
    peers = lax.axis_size("seq")
    at = lax.axis_index("seq")
    odd = (at & 1) != 0
    rows = tokens // n
    me_array = jnp.full((1,), me, jnp.int32)

    order = to_relative(jnp.arange(tokens, dtype=jnp.int32), me, n)
    starts_here = to_relative(starts, me, n)
    positions = (at * tokens + order - starts_here).astype(F32)
    freqs = 10000.0 ** (-2.0 * jnp.arange(HEAD // 2, dtype=F32) / HEAD)
    angles = positions[:, None] * freqs[None, :]
    cosine, sine = jnp.cos(angles), jnp.sin(angles)
    cosine, sine = jnp.concatenate([cosine, cosine], 1), jnp.concatenate([-sine, sine], 1)
    low = jnp.maximum(starts_here - (at - 2) * tokens, order + 2 * tokens - WINDOW + 1)[None, :]

    hidden_one, query, key, value = qkv(
        me_array, block_input, norm_one[None, :], w_query, w_key, w_value, cosine, sine, n
    )

    right_two = [(i, i + 2) for i in range(peers - 2)]
    left_two = [(i + 2, i) for i in range(peers - 2)]
    to_odd = [(i, i + 1) for i in range(0, peers, 2)]
    to_even = [(i + 1, i) for i in range(0, peers, 2)]
    packed = jnp.stack([key, value])
    before_two = lax.ppermute(packed, "seq", right_two)
    across = lax.ppermute(packed, "seq", to_odd)
    before_one = jnp.where(odd, across, lax.ppermute(before_two, "seq", to_even))
    window = jnp.concatenate([before_two, before_one, packed], axis=1)
    keys, values = window[0], window[1]

    attended, lse = attend(me_array, query, keys, values, low, n)
    attn_part = mm(attended, w_out).astype(BF16)
    input_own = lax.dynamic_slice_in_dim(block_input, me * rows, rows, 0).astype(F32)
    cot_own = lax.dynamic_slice_in_dim(cotangent, me * rows, rows, 0).astype(F32)
    cot = to_relative(cotangent, me, n)
    d_act = mm(cot, w_down, NT)

    mid = input_own + sum_blocks(attn_part, n)
    r_two = lax.rsqrt(jnp.mean(mid * mid, axis=-1, keepdims=True) + 1e-06)
    n_two = mid * r_two
    hidden_two = jnp.concatenate(all_blocks((n_two * norm_two).astype(BF16), n), axis=0)

    gate = mm(hidden_two, w_gate)
    up = mm(hidden_two, w_up)
    s = 1.0 / (1.0 + jnp.exp(-gate))
    silu = gate * s
    activation = (silu * up).astype(BF16)
    d_gate = (d_act * up * s * (1.0 + gate * (1.0 - s))).astype(BF16)
    d_up = (d_act * silu).astype(BF16)
    d_two_part = (mm(d_gate, w_gate, NT) + mm(d_up, w_up, NT)).astype(BF16)
    d_hidden_two = sum_blocks(d_two_part, n)
    e_two = d_hidden_two * norm_two
    d_mid = cot_own + r_two * (e_two - n_two * jnp.mean(e_two * n_two, axis=-1, keepdims=True))
    d_mid_low = jnp.concatenate(all_blocks(d_mid.astype(BF16), n), axis=0)

    mlp_part = mm(activation, w_down).astype(BF16)
    grad_down = scattered(mm(activation, cot, TN), 1)
    grad_gate = scattered(mm(hidden_two, d_gate, TN), 0)
    grad_up = scattered(mm(hidden_two, d_up, TN), 0)
    out_own = (mid + sum_blocks(mlp_part, n)).astype(BF16)
    output = to_natural(all_blocks(out_own, n), me)

    d_attended = mm(d_mid_low, w_out, NT).astype(BF16)
    grad_out = scattered(mm(attended, d_mid_low, TN), 1)
    d_query, d_keys, d_values = attend_back(
        me_array, query, keys, values, low, attended, d_attended, lse, cosine, sine, n
    )
    d_window = jnp.stack([d_keys, d_values])
    d_two_back, d_one_back, d_own = (
        d_window[:, :tokens], d_window[:, tokens : 2 * tokens], d_window[:, 2 * tokens :],
    )
    d_across = swap(d_one_back, 1, "seq").astype(F32)
    sent = (d_two_back.astype(F32) + jnp.where(odd, d_across, 0.0)).astype(BF16)
    d_own = d_own.astype(F32) + jnp.where(odd, 0.0, d_across)
    d_own = d_own + lax.ppermute(sent, "seq", left_two).astype(F32)
    d_key = rotate_wide(d_own[0], cosine, -sine).astype(BF16)
    d_value = d_own[1].astype(BF16)

    d_one_part = (
        mm(d_query, w_query, NT) + mm(d_key, w_key, NT) + mm(d_value, w_value, NT)
    ).astype(BF16)
    d_hidden_one = sum_blocks(d_one_part, n)
    grad_query = scattered(mm(hidden_one, d_query, TN), 0)
    grad_key = scattered(mm(hidden_one, d_key, TN), 0)
    grad_value = scattered(mm(hidden_one, d_value, TN), 0)

    r_one = lax.rsqrt(jnp.mean(input_own * input_own, axis=-1, keepdims=True) + 1e-06)
    n_one = input_own * r_one
    e_one = d_hidden_one * norm_one
    input_grad = d_mid + r_one * (e_one - n_one * jnp.mean(e_one * n_one, axis=-1, keepdims=True))
    others = all_blocks(input_grad.astype(BF16), n)[1:]
    grad_input = to_natural([input_grad] + [b.astype(F32) for b in others], me)
    gains = gain_sums(
        jnp.stack([jnp.sum(d_hidden_one * n_one, 0), jnp.sum(d_hidden_two * n_two, 0)]), n
    )
    return (
        output, grad_input, gains[0], grad_query, grad_key, grad_value, grad_out, gains[1],
        grad_gate, grad_up, grad_down,
    )


def solution(mesh):
    in_specs = (
        P("seq", None), P(), P(None, "tp"), P(None, "tp"), P(None, "tp"), P("tp", None), P(),
        P(None, "tp"), P(None, "tp"), P("tp", None), P("seq"), P("seq", None),
    )
    out_specs = (
        P("seq", None), P("seq", None), P("seq"), P("seq", "tp"), P("seq", "tp"), P("seq", "tp"),
        P("tp", "seq"), P("seq"), P("seq", "tp"), P("seq", "tp"), P("tp", "seq"),
    )
    return jax.shard_map(
        on_device, mesh=mesh, in_specs=in_specs, out_specs=out_specs, check_vma=False
    )
```

```python
import jax
import jax.numpy as jnp
from jax import lax
from jax.experimental import pallas as pl
from jax.experimental.pallas import tpu as pltpu
from jax.sharding import PartitionSpec as P

HEAD = 128
WINDOW = 2048
LOG2E = 1.4426950408889634
SCALE = HEAD ** (-0.5)
NEG = -1e30
F32 = jnp.float32
BF16 = jnp.bfloat16
MIB = 1024 * 1024
GROUPS = 2

NN = (((1,), (0,)), ((), ()))
NT = (((1,), (1,)), ((), ()))
TN = (((0,), (0,)), ((), ()))


def mm(a, b, dims=NN):
    return lax.dot_general(a, b, dims, preferred_element_type=F32)


def tied(values, after):
    return lax.optimization_barrier((values, after))[0]


def call(body, grid, in_specs, out_specs, outs, args, name, scratch=(), flops=0, moved=0, exps=0, vmem=48):
    return pl.pallas_call(
        body,
        grid_spec=pltpu.PrefetchScalarGridSpec(
            num_scalar_prefetch=1,
            grid=grid,
            in_specs=in_specs,
            out_specs=out_specs,
            scratch_shapes=list(scratch),
        ),
        out_shape=[jax.ShapeDtypeStruct(shape, kind) for shape, kind in outs],
        compiler_params=pltpu.CompilerParams(vmem_limit_bytes=vmem * MIB),
        cost_estimate=pl.CostEstimate(flops=0, bytes_accessed=0, transcendentals=0),
        name=name,
    )(*args)


def fixed(shape):
    return pl.BlockSpec(shape, lambda *_: (0,) * len(shape), pipeline_mode=pl.Buffered(1))


def to_relative(array, me, n):
    rows = array.shape[0] // n
    return jnp.concatenate(
        [lax.dynamic_slice_in_dim(array, (r ^ me) * rows, rows, 0) for r in range(n)], axis=0
    )


def swap(array, bit, axis="tp"):
    size = lax.axis_size(axis)
    return lax.ppermute(array, axis, [(i, i ^ bit) for i in range(size)])


def bits_of(n):
    return [1 << b for b in range(n.bit_length() - 1)]


def sum_first(parts, n):
    cut = lambda r, side: parts[2 * r + side]
    if n == 4:
        three_left, three_right = swap(cut(3, 0), 1), swap(cut(3, 1), 2)
        one_left, two_right = swap(cut(1, 0), 1), swap(cut(2, 1), 2)
        one_right = (cut(1, 1).astype(F32) + three_right.astype(F32)).astype(BF16)
        two_left = (cut(2, 0).astype(F32) + three_left.astype(F32)).astype(BF16)
        return (one_right, two_left), ([cut(0, 0), one_left], [cut(0, 1), two_right])
    sides = []
    rows = parts[0].shape[0]
    for side, order in enumerate((bits_of(n), bits_of(n)[::-1])):
        held = {r: cut(r, side) for r in range(n)}
        for bit in order:
            sent = [r for r in held if r & bit]
            got = swap(jnp.concatenate([held[r] for r in sent]).astype(BF16), bit)
            held = {
                r ^ bit: held[r ^ bit].astype(F32) + got[k * rows : (k + 1) * rows].astype(F32)
                for k, r in enumerate(sent)
            }
        sides.append(held[0])
    return tuple(sides), ([], [])


def sum_second(sent, kept, n):
    if n == 4:
        one_right, two_left = swap(sent[0], 1), swap(sent[1], 2)
        return kept[0] + [two_left], kept[1] + [one_right]
    return [sent[0]], [sent[1]]


def all_blocks(own, n):
    left, right = own
    if n == 4:
        one_right, two_left = swap(right, 1), swap(left, 2)
        one_left, two_right = swap(left, 1), swap(right, 2)
        three_left, three_right = swap(two_left, 1), swap(one_right, 2)
        return [left, one_left, two_left, three_left], [right, one_right, two_right, three_right]
    sides = []
    rows = left.shape[0]
    for side, order in enumerate((bits_of(n)[::-1], bits_of(n))):
        held = {0: own[side]}
        for bit in order:
            have = sorted(held)
            got = swap(jnp.concatenate([held[r] for r in have]), bit)
            for k, r in enumerate(have):
                held[r ^ bit] = got[k * rows : (k + 1) * rows]
        sides.append([held[r] for r in range(n)])
    return sides[0], sides[1]


def rotated(a, cosine, sine):
    return a * cosine + pltpu.roll(a, HEAD // 2, 1) * sine


def total(refs):
    out = refs[0][...].astype(F32)
    for ref in refs[1:]:
        out = out + ref[...].astype(F32)
    return out


def heads_of(width):
    return [slice(h * HEAD, (h + 1) * HEAD) for h in range(width // HEAD)]


def keys_kernel(me_ref, x_ref, gain_ref, wk_ref, wv_ref, cos_ref, sin_ref, h_ref, *kv_refs):
    x = x_ref[...].astype(F32)
    factor = lax.rsqrt(jnp.mean(x * x, axis=-1, keepdims=True) + 1e-06)
    hidden = (x * factor * gain_ref[...]).astype(BF16)
    h_ref[...] = hidden
    cosine, sine = cos_ref[...], sin_ref[...]
    for g, kv_ref in enumerate(kv_refs):
        width = kv_ref.shape[2]
        cols = slice(g * width, (g + 1) * width)
        key = mm(hidden, wk_ref[:, cols])
        for cut in heads_of(width):
            kv_ref[0, :, cut] = rotated(key[:, cut], cosine, sine).astype(BF16)
        kv_ref[1] = mm(hidden, wv_ref[:, cols]).astype(BF16)


def project_keys(scal, x, gain, wk, wv, cosine, sine, n):
    tokens, width = x.shape
    local = wk.shape[1]
    rows, part = tokens // n, local // GROUPS
    mine = lambda r, m: (r, 0)
    return call(
        keys_kernel,
        (n,),
        [
            pl.BlockSpec((rows, width), lambda r, m: (r ^ m[0], 0)),
            fixed((1, width)),
            fixed((width, local)),
            fixed((width, local)),
            pl.BlockSpec((rows, HEAD), mine),
            pl.BlockSpec((rows, HEAD), mine),
        ],
        [pl.BlockSpec((rows, width), mine)]
        + [pl.BlockSpec((2, rows, part), lambda r, m: (0, r, 0))] * GROUPS,
        [((tokens, width), BF16)] + [((2, tokens, part), BF16)] * GROUPS,
        (scal, x, gain, wk, wv, cosine, sine),
        "project_keys",
        flops=4 * tokens * width * local,
        moved=4 * tokens * width + 4 * (tokens + width) * local,
    )


def query_kernel(me_ref, h_ref, w_ref, cos_ref, sin_ref, q_ref):
    pre = mm(h_ref[...], w_ref[...])
    for cut in heads_of(pre.shape[1]):
        q_ref[:, cut] = rotated(pre[:, cut], cos_ref[...], sin_ref[...]).astype(BF16)


def project_query(scal, hidden, wq, cosine, sine, n):
    tokens, width = hidden.shape
    local = wq.shape[1]
    rows = tokens // n
    mine = lambda r, m: (r, 0)
    return call(
        query_kernel,
        (n,),
        [
            pl.BlockSpec((rows, width), mine),
            fixed((width, local)),
            pl.BlockSpec((rows, HEAD), mine),
            pl.BlockSpec((rows, HEAD), mine),
        ],
        [pl.BlockSpec((rows, local), mine)],
        [((tokens, local), BF16)],
        (scal, hidden, wq, cosine, sine),
        "project_query",
        flops=2 * tokens * width * local,
        moved=2 * tokens * width + 2 * (tokens + width) * local,
    )[0]


def act_kernel(me_ref, cot_ref, w_ref, rel_ref, d_ref):
    cot = cot_ref[...]
    rel_ref[...] = cot
    d_ref[...] = mm(cot, w_ref[...], NT)


def project_cotangent(scal, cot, w_down, n):
    tokens, width = cot.shape
    hid = w_down.shape[0]
    rows = tokens // n
    mine = lambda r, m: (r, 0)
    return call(
        act_kernel,
        (n,),
        [pl.BlockSpec((rows, width), lambda r, m: (r ^ m[0], 0)), fixed((hid, width))],
        [pl.BlockSpec((rows, width), mine), pl.BlockSpec((rows, hid), mine)],
        [((tokens, width), BF16), ((tokens, hid), F32)],
        (scal, cot, w_down),
        "project_cotangent",
        flops=2 * tokens * width * hid,
        moved=4 * tokens * width + 4 * tokens * hid + 2 * width * hid,
    )


def masked(s, first, low, query_at, diagonal):
    key_at = first + lax.broadcasted_iota(jnp.int32, s.shape, 0)
    keep = key_at >= low
    if diagonal:
        keep = keep & (key_at <= query_at)
    return jnp.where(keep, s, NEG)


def lay_window(n, rows, me, odd, which, two_ref, odd_ref, even_ref, own_ref, put):
    for seg, refs in enumerate(((two_ref,), (odd_ref, even_ref), (own_ref,))):
        for sub in range(n):
            here = pl.ds(pl.multiple_of((sub ^ me) * rows, rows), rows)
            at = slice((seg * n + sub) * rows, (seg * n + sub + 1) * rows)
            if len(refs) == 1:
                put(at, refs[0][which, here, :])
            else:
                put(at, jnp.where(odd != 0, refs[0][which, here, :], refs[1][which, here, :]))


def attend_kernel(n, s_ref_, q_ref, two_ref, odd_ref, even_ref, own_ref, low_ref, o_ref, lse_ref, s_ref, k_ref, vt_ref):
    rows = q_ref.shape[0]
    me, odd = s_ref_[0], s_ref_[1]
    r = pl.program_id(1)
    rb = r ^ me
    chunks = 2 * n + 1

    @pl.when(r == 0)
    def _():
        def put_key(at, block):
            k_ref[at, :] = block

        def put_value(at, block):
            vt_ref[:, at] = block.T

        window = (two_ref, odd_ref, even_ref, own_ref)
        lay_window(n, rows, me, odd, 0, *window, put_key)
        lay_window(n, rows, me, odd, 1, *window, put_value)

    q = q_ref[...]
    low = low_ref[...]
    query_at = (rb + 2 * n) * rows + lax.broadcasted_iota(jnp.int32, (1, rows), 1)
    top = jnp.full((1, rows), NEG, F32)
    for c in range(chunks):
        first = pl.multiple_of((rb + c) * rows, rows)
        s = mm(k_ref[pl.ds(first, rows), :], q, NT)
        s = masked(s, first, low, query_at, c == chunks - 1)
        s_ref[c * rows : (c + 1) * rows, :] = s
        top = jnp.maximum(top, jnp.max(s, axis=0, keepdims=True))
    top = top * (SCALE * LOG2E)
    whole = jnp.zeros((1, rows), F32)
    acc = jnp.zeros((HEAD, rows), F32)
    for c in range(chunks):
        first = pl.multiple_of((rb + c) * rows, rows)
        p = jnp.exp2(s_ref[c * rows : (c + 1) * rows, :] * (SCALE * LOG2E) - top)
        whole = whole + jnp.sum(p, axis=0, keepdims=True)
        acc = acc + mm(vt_ref[:, pl.ds(first, rows)], p.astype(BF16))
    o_ref[...] = (acc / whole).T.astype(BF16)
    lse_ref[...] = (top + jnp.log2(whole)).reshape(lse_ref.shape)


def attend(scal, g, q, segments, low, n):
    tokens = q.shape[0]
    part = segments[0].shape[2]
    heads, rows = part // HEAD, tokens // n
    pairs = heads * tokens * (2 * tokens + rows)
    segment = pl.BlockSpec((2, tokens, HEAD), lambda h, r, m: (0, 0, h))
    return call(
        lambda *refs: attend_kernel(n, *refs),
        (heads, n),
        [pl.BlockSpec((rows, HEAD), lambda h, r, m: (r, g * heads + h))]
        + [segment] * 4
        + [pl.BlockSpec((1, rows), lambda h, r, m: (0, r))],
        [
            pl.BlockSpec((rows, HEAD), lambda h, r, m: (r, h)),
            pl.BlockSpec((1, 1, rows), lambda h, r, m: (h, 0, r)),
        ],
        [((tokens, part), BF16), ((heads, 1, tokens), F32)],
        (scal, q, *segments, low),
        "attend",
        scratch=[
            pltpu.VMEM(((2 * n + 1) * rows, rows), F32),
            pltpu.VMEM((3 * tokens, HEAD), BF16),
            pltpu.VMEM((HEAD, 3 * tokens), BF16),
        ],
        flops=8 * pairs * HEAD,
        moved=20 * tokens * part,
        exps=pairs,
    )


def attend_back_kernel(
    n, s_ref_, q_ref, two_ref, odd_ref, even_ref, own_ref, low_ref, o_ref, do_ref, lse_ref, cos_ref, sin_ref,
    dq_ref, d_two_ref, d_one_ref, d_own_ref, dk_acc, dv_acc, k_ref, kt_ref, v_ref,
):
    rows = q_ref.shape[0]
    me, odd = s_ref_[0], s_ref_[1]
    r = pl.program_id(1)
    rb = r ^ me
    chunks = 2 * n + 1

    @pl.when(r == 0)
    def _():
        def put_key(at, block):
            k_ref[at, :] = block
            kt_ref[:, at] = block.T
            dk_acc[at, :] = jnp.zeros((rows, HEAD), F32)
            dv_acc[at, :] = jnp.zeros((rows, HEAD), F32)

        def put_value(at, block):
            v_ref[at, :] = block

        window = (two_ref, odd_ref, even_ref, own_ref)
        lay_window(n, rows, me, odd, 0, *window, put_key)
        lay_window(n, rows, me, odd, 1, *window, put_value)

    q, do = q_ref[...], do_ref[...]
    low = low_ref[...]
    lse = lse_ref[...].reshape(1, rows)
    delta = jnp.sum((do.astype(F32) * o_ref[...].astype(F32)).T, axis=0, keepdims=True)
    query_at = (rb + 2 * n) * rows + lax.broadcasted_iota(jnp.int32, (1, rows), 1)
    dqt = jnp.zeros((HEAD, rows), F32)
    for c in range(chunks):
        first = pl.multiple_of((rb + c) * rows, rows)
        here = pl.ds(first, rows)
        s = mm(k_ref[here, :], q, NT) * (SCALE * LOG2E)
        s = masked(s, first, low, query_at, c == chunks - 1)
        p = jnp.exp2(s - lse)
        dv_acc[here, :] += mm(p.astype(BF16), do)
        dp = mm(v_ref[here, :], do, NT)
        ds = (p * (dp - delta)).astype(BF16)
        dk_acc[here, :] += mm(ds, q)
        dqt = dqt + mm(kt_ref[:, here], ds)
    dq_ref[...] = rotated(dqt.T * SCALE, cos_ref[...], -sin_ref[...]).astype(BF16)

    @pl.when(r == n - 1)
    def _():
        for seg, out_ref in enumerate((d_two_ref, d_one_ref, d_own_ref)):
            for sub in range(n):
                here = pl.ds(pl.multiple_of((sub ^ me) * rows, rows), rows)
                at = slice((seg * n + sub) * rows, (seg * n + sub + 1) * rows)
                out_ref[0, here, :] = (dk_acc[at, :] * SCALE).astype(BF16)
                out_ref[1, here, :] = dv_acc[at, :].astype(BF16)


def attend_back(scal, g, q, segments, low, attended, d_attended, lse, cosine, sine, n):
    tokens = q.shape[0]
    part = segments[0].shape[2]
    heads, rows = part // HEAD, tokens // n
    pairs = heads * tokens * (2 * tokens + rows)
    block = pl.BlockSpec((rows, HEAD), lambda h, r, m: (r, h))
    shared = pl.BlockSpec((rows, HEAD), lambda h, r, m: (r, g * heads + h))
    segment = pl.BlockSpec((2, tokens, HEAD), lambda h, r, m: (0, 0, h))
    table = pl.BlockSpec((rows, HEAD), lambda h, r, m: (r, 0))
    return call(
        lambda *refs: attend_back_kernel(n, *refs),
        (heads, n),
        [shared]
        + [segment] * 4
        + [
            pl.BlockSpec((1, rows), lambda h, r, m: (0, r)),
            block,
            shared,
            pl.BlockSpec((1, 1, rows), lambda h, r, m: (h, 0, r)),
            table,
            table,
        ],
        [block] + [segment] * 3,
        [((tokens, part), BF16)] + [((2, tokens, part), BF16)] * 3,
        (scal, q, *segments, low, attended, d_attended, lse, cosine, sine),
        "attend_back",
        scratch=[
            pltpu.VMEM((3 * tokens, HEAD), F32),
            pltpu.VMEM((3 * tokens, HEAD), F32),
            pltpu.VMEM((3 * tokens, HEAD), BF16),
            pltpu.VMEM((HEAD, 3 * tokens), BF16),
            pltpu.VMEM((3 * tokens, HEAD), BF16),
        ],
        flops=20 * pairs * HEAD,
        moved=36 * tokens * part,
        exps=pairs,
    )


def put_part(value, refs):
    half = refs[0].shape[1]
    value = value.astype(BF16)
    for r in range(len(refs) // 2):

        @pl.when(pl.program_id(0) == r)
        def _():
            refs[2 * r][...] = value[:, :half]
            refs[2 * r + 1][...] = value[:, half:]


def part_outs(n, rows, width):
    half = (rows, width // 2)
    return [pl.BlockSpec(half, lambda *_: (0, 0))] * (2 * n), [(half, BF16)] * (2 * n)


def sum_kernel(count, me_ref, *refs):
    arrays, w_ref, part_refs = refs[:count], refs[count], refs[count + 1 :]
    deep = arrays[0].shape[1]
    acc = mm(arrays[0][...], w_ref[:deep, :])
    for g in range(1, count):
        acc = acc + mm(arrays[g][...], w_ref[g * deep : (g + 1) * deep, :])
    put_part(acc, part_refs)


def project_sum(scal, arrays, weight, n, name):
    tokens, deep = arrays[0].shape
    width = weight.shape[1]
    rows = tokens // n
    specs, outs = part_outs(n, rows, width)
    return call(
        lambda *refs: sum_kernel(len(arrays), *refs),
        (n,),
        [pl.BlockSpec((rows, deep), lambda r, m: (r, 0))] * len(arrays) + [fixed(weight.shape)],
        specs,
        outs,
        (scal, *arrays, weight),
        name,
    )


def own_rows(kernel, scal, outs, args, lists, name):
    rows, half = lists[0][0].shape
    flat = tuple(lists[0]) + tuple(lists[1])
    count = len(args)

    def body(_, *refs):
        left = refs[count : count + len(lists[0])]
        right = refs[count + len(lists[0]) : count + len(flat)]
        summed = jnp.concatenate([total(left), total(right)], axis=1)
        kernel(summed, *refs[:count], *refs[count + len(flat) :])

    own = pl.BlockSpec((rows, 2 * half), lambda i, m: (m[0], 0))
    return call(
        body,
        (1,),
        [own if a.shape[0] > rows else fixed(a.shape) for a in args] + [fixed((rows, half))] * len(flat),
        [fixed(shape) for shape, _ in outs],
        outs,
        (scal, *args, *flat),
        name,
    )


def mid_kernel(summed, x_ref, gain_ref, mid_ref, left_ref, right_ref):
    half = left_ref.shape[1]
    mid = x_ref[...].astype(F32) + summed
    mid_ref[...] = mid
    factor = lax.rsqrt(jnp.mean(mid * mid, axis=-1, keepdims=True) + 1e-06)
    hidden = (mid * factor * gain_ref[...]).astype(BF16)
    left_ref[...] = hidden[:, :half]
    right_ref[...] = hidden[:, half:]


def back_norm(d_hidden, values, gain, d_gain_ref=None):
    factor = lax.rsqrt(jnp.mean(values * values, axis=-1, keepdims=True) + 1e-06)
    normed = values * factor
    if d_gain_ref is not None:
        d_gain_ref[...] = jnp.sum(d_hidden * normed, axis=0, keepdims=True)
    e = d_hidden * gain
    return factor * (e - normed * jnp.mean(e * normed, axis=-1, keepdims=True))


def d_mid_kernel(d_hidden, mid_ref, gain_ref, cot_ref, d_mid_ref, left_ref, right_ref, d_gain_ref):
    half = left_ref.shape[1]
    d_mid = cot_ref[...].astype(F32) + back_norm(d_hidden, mid_ref[...], gain_ref[...], d_gain_ref)
    d_mid_ref[...] = d_mid
    left_ref[...] = d_mid[:, :half].astype(BF16)
    right_ref[...] = d_mid[:, half:].astype(BF16)


def input_kernel(d_hidden, x_ref, gain_ref, d_mid_ref, own_ref, left_ref, right_ref):
    half = left_ref.shape[1]
    grad = d_mid_ref[...] + back_norm(d_hidden, x_ref[...].astype(F32), gain_ref[...])
    own_ref[...] = grad
    left_ref[...] = grad[:, :half].astype(BF16)
    right_ref[...] = grad[:, half:].astype(BF16)


def output_kernel(summed, mid_ref, left_ref, right_ref):
    half = left_ref.shape[1]
    out = (mid_ref[...] + summed).astype(BF16)
    left_ref[...] = out[:, :half]
    right_ref[...] = out[:, half:]


def lay_block(n, left_refs, right_refs, whole_ref):
    half = left_refs[0].shape[1]
    for r in range(n):

        @pl.when(pl.program_id(0) == r)
        def _():
            whole_ref[:, :half] = left_refs[r][...].astype(whole_ref.dtype)
            whole_ref[:, half:] = right_refs[r][...].astype(whole_ref.dtype)


def mlp_kernel(n, me_ref, *refs):
    left, right = refs[:n], refs[n : 2 * n]
    d_act_ref, wg_ref, wu_ref, h_ref, act_ref, dg_ref, du_ref = refs[2 * n : 2 * n + 7]
    lay_block(n, left, right, h_ref)
    hidden = h_ref[...]
    gate = mm(hidden, wg_ref[...], NT)
    up = mm(hidden, wu_ref[...], NT)
    d_act = d_act_ref[...]
    s = 1.0 / (1.0 + jnp.exp(-gate))
    silu = gate * s
    act_ref[...] = (silu * up).astype(BF16)
    d_gate = (d_act * up * s * (1.0 + gate * (1.0 - s))).astype(BF16)
    d_up = (d_act * silu).astype(BF16)
    dg_ref[...] = d_gate
    du_ref[...] = d_up
    put_part(mm(d_gate, wg_ref[...]) + mm(d_up, wu_ref[...]), refs[2 * n + 7 :])


def mlp(scal, halves, d_act, w_gate, w_up, n):
    rows, half = halves[0][0].shape
    hid, width = w_gate.shape
    tokens = rows * n
    mine = lambda r, m: (r, 0)
    specs, outs = part_outs(n, rows, width)
    hidden, act, d_gate, d_up, *parts = call(
        lambda *refs: mlp_kernel(n, *refs),
        (n,),
        [fixed((rows, half))] * (2 * n)
        + [pl.BlockSpec((rows, hid), mine), fixed((hid, width)), fixed((hid, width))],
        [pl.BlockSpec((rows, width), mine)] + [pl.BlockSpec((rows, hid), mine)] * 3 + specs,
        [((tokens, width), BF16)] + [((tokens, hid), BF16)] * 3 + outs,
        (scal, *halves[0], *halves[1], d_act, w_gate, w_up),
        "mlp",
        vmem=56,
    )
    return hidden, act, d_gate, d_up, parts


def d_attended_kernel(n, me_ref, *refs):
    left, right = refs[:n], refs[n : 2 * n]
    w_ref, low_ref, d_ref = refs[2 * n :]
    lay_block(n, left, right, low_ref)
    d_ref[...] = mm(low_ref[...], w_ref[...], NT).astype(BF16)


def project_back(scal, halves, w_out, n):
    rows, half = halves[0][0].shape
    local, width = w_out.shape
    tokens = rows * n
    mine = lambda r, m: (r, 0)
    return call(
        lambda *refs: d_attended_kernel(n, *refs),
        (n,),
        [fixed((rows, half))] * (2 * n) + [fixed((local, width))],
        [pl.BlockSpec((rows, width), mine), pl.BlockSpec((rows, local), mine)],
        [((tokens, width), BF16), ((tokens, local), BF16)],
        (scal, *halves[0], *halves[1], w_out),
        "project_back",
        flops=2 * tokens * width * local,
        moved=4 * tokens * width + 2 * (tokens + width) * local,
    )


def place_kernel(blocks, has_own, me_ref, *refs):
    count = len(blocks)
    left, right, out_ref = refs[:count], refs[count : 2 * count], refs[-1]
    lay_block(count, left, right, out_ref)
    if has_own:

        @pl.when(pl.program_id(0) == 0)
        def _():
            out_ref[...] = refs[2 * count][...]


def place(scal, halves, blocks, kind, n, own=None, whole=None):
    rows, half = halves[0][0].shape
    first = blocks[0]
    arrays = [side[r] for side in halves for r in blocks]
    extra = [] if own is None else [own]
    held = [] if whole is None else [whole]
    return pl.pallas_call(
        lambda *refs: place_kernel(blocks, own is not None, *refs),
        grid_spec=pltpu.PrefetchScalarGridSpec(
            num_scalar_prefetch=1,
            grid=(len(blocks),),
            in_specs=[fixed((rows, half))] * len(arrays)
            + [fixed(e.shape) for e in extra]
            + [pl.BlockSpec(memory_space=pl.ANY)] * len(held),
            out_specs=pl.BlockSpec((rows, 2 * half), lambda r, m: ((r + first) ^ m[0], 0)),
        ),
        out_shape=jax.ShapeDtypeStruct((rows * n, 2 * half), kind),
        input_output_aliases={1 + len(arrays) + len(extra): 0} if held else {},
        compiler_params=pltpu.CompilerParams(vmem_limit_bytes=40 * MIB),
        cost_estimate=pl.CostEstimate(flops=0, bytes_accessed=0, transcendentals=0),
        name="place",
    )(scal, *arrays, *extra, *held)


def finish_kernel(s_ref_, own_ref, across_ref, back_ref, dq_ref, cos_ref, sin_ref, all_ref):
    part = dq_ref.shape[1]
    share = jnp.where(s_ref_[1] != 0, 0.0, 1.0)
    whole = own_ref[...].astype(F32) + back_ref[...].astype(F32) + across_ref[...].astype(F32) * share
    all_ref[:, :part] = dq_ref[...]
    for h, cut in enumerate(heads_of(part)):
        to = slice(part + h * HEAD, part + (h + 1) * HEAD)
        all_ref[:, to] = rotated(whole[0, :, cut], cos_ref[...], -sin_ref[...]).astype(BF16)
    all_ref[:, 2 * part :] = whole[1].astype(BF16)


def finish(scal, own, across, back, dq, cosine, sine, n):
    tokens, part = dq.shape
    rows = tokens // n
    segment = pl.BlockSpec((2, rows, part), lambda r, m: (0, r, 0))
    mine = lambda r, m: (r, 0)
    return call(
        finish_kernel,
        (n,),
        [segment] * 3
        + [pl.BlockSpec((rows, part), mine), pl.BlockSpec((rows, HEAD), mine), pl.BlockSpec((rows, HEAD), mine)],
        [pl.BlockSpec((rows, 3 * part), mine)],
        [((tokens, 3 * part), BF16)],
        (scal, own, across, back, dq, cosine, sine),
        "finish",
        moved=20 * tokens * part,
    )[0]


def d_one_kernel(me_ref, *refs):
    grads, weights = refs[:GROUPS], refs[GROUPS : GROUPS + 3]
    x_ref, gain_ref = refs[GROUPS + 3 : GROUPS + 5]
    part = grads[0].shape[1] // 3
    acc = None
    for g, grad in enumerate(grads):
        for k, w_ref in enumerate(weights):
            term = mm(grad[:, k * part : (k + 1) * part], w_ref[:, g * part : (g + 1) * part], NT)
            acc = term if acc is None else acc + term
    put_part(acc, refs[GROUPS + 5 :])
    x = x_ref[...].astype(F32)
    factor = lax.rsqrt(jnp.mean(x * x, axis=-1, keepdims=True) + 1e-06)

    @pl.when(pl.program_id(0) == 0)
    def _():
        gain_ref[...] = jnp.zeros_like(gain_ref)

    gain_ref[...] += jnp.sum(acc * (x * factor), axis=0, keepdims=True)


def project_one_back(scal, grads, weights, x, n):
    tokens, triple = grads[0].shape
    width, local = weights[0].shape
    rows = tokens // n
    specs, outs = part_outs(n, rows, width)
    d_gain, *parts = call(
        d_one_kernel,
        (n,),
        [pl.BlockSpec((rows, triple), lambda r, m: (r, 0))] * GROUPS
        + [fixed((width, local))] * 3
        + [pl.BlockSpec((rows, width), lambda r, m: (r ^ m[0], 0))],
        [fixed((1, width))] + specs,
        [((1, width), F32)] + outs,
        (scal, *grads, *weights, x),
        "project_one_back",
    )
    return d_gain, parts


def seq_sums(sums):
    peers = lax.axis_size("seq")
    at = lax.axis_index("seq")
    for bit in bits_of(peers)[::-1]:
        half = sums.shape[1] // 2
        upper = (at & bit) != 0
        low_part, high_part = sums[:, :half], sums[:, half:]
        kept = jnp.where(upper, high_part, low_part)
        sums = kept + swap(jnp.where(upper, low_part, high_part), bit, "seq")
    return sums


def scattered(grad, dim):
    return lax.psum_scatter(grad, "seq", scatter_dimension=dim, tiled=True)


def on_device(
    block_input, norm_one, w_query, w_key, w_value, w_out, norm_two, w_gate, w_up, w_down,
    starts, cotangent,
):
    tokens, width = block_input.shape
    hid = w_gate.shape[1]
    n = lax.axis_size("tp")
    me = lax.axis_index("tp")
    peers = lax.axis_size("seq")
    at = lax.axis_index("seq")
    rows = tokens // n
    odd = (at & 1) != 0
    scal = jnp.stack([me, at & 1]).astype(jnp.int32)
    gain_one, gain_two = norm_one[None, :], norm_two[None, :]

    order = to_relative(jnp.arange(tokens, dtype=jnp.int32), me, n)
    starts_here = to_relative(starts, me, n)
    positions = (at * tokens + order - starts_here).astype(F32)
    freqs = 10000.0 ** (-2.0 * jnp.arange(HEAD // 2, dtype=F32) / HEAD)
    angles = positions[:, None] * freqs[None, :]
    cosine, sine = jnp.cos(angles), jnp.sin(angles)
    cosine, sine = jnp.concatenate([cosine, cosine], 1), jnp.concatenate([-sine, sine], 1)
    low = jnp.maximum(starts_here - (at - 2) * tokens, order + 2 * tokens - WINDOW + 1)[None, :]

    hidden_one, *packed = project_keys(scal, block_input, gain_one, w_key, w_value, cosine, sine, n)

    right_two = [(i, i + 2) for i in range(peers - 2)]
    left_two = [(i + 2, i) for i in range(peers - 2)]
    to_odd = [(i, i + 1) for i in range(0, peers, 2)]
    to_even = [(i + 1, i) for i in range(0, peers, 2)]
    query = project_query(scal, hidden_one, w_query, cosine, sine, n)
    cot, d_act = project_cotangent(scal, cotangent, w_down, n)

    segments, attended, lse = [], [], []
    twos = [lax.ppermute(own, "seq", right_two) for own in packed]
    acrosses = [lax.ppermute(own, "seq", to_odd) for own in packed]
    for g, own in enumerate(packed):
        two = tied(twos[g], attended[g - 1] if g else (query, d_act))
        segments.append((two, acrosses[g], lax.ppermute(two, "seq", to_even), own))
        out, peak = attend(scal, g, query, segments[g], low, n)
        attended.append(out)
        lse.append(peak)
    parts = project_sum(scal, attended, w_out, n, "project_out")
    own_f32, own_half = ((rows, width), F32), ((rows, width // 2), BF16)
    mid, *hidden_own = own_rows(
        mid_kernel, scal, [own_f32, own_half, own_half], (block_input, gain_two),
        sum_second(*sum_first(parts, n), n), "mid",
    )
    hidden_halves = all_blocks(hidden_own, n)
    hidden_two, activation, d_gate, d_up, parts = mlp(scal, hidden_halves, d_act, w_gate.T, w_up.T, n)

    d_two_sent, d_two_kept = sum_first(parts, n)
    d_two_sent, act_later, d_gate_later = lax.optimization_barrier((d_two_sent, activation, d_gate))
    d_hidden_two = sum_second(d_two_sent, d_two_kept, n)
    grad_down = mm(act_later, cot, TN).astype(BF16)
    grad_gate = mm(d_gate_later, hidden_two, TN).astype(BF16)
    d_hidden_two, grad_down, grad_gate = lax.optimization_barrier((d_hidden_two, grad_down, grad_gate))
    grad_down, grad_gate = scattered(grad_down, 1), scattered(grad_gate, 1)
    gain_row = ((1, width), F32)
    d_mid, *d_mid_own, d_gain_two = own_rows(
        d_mid_kernel, scal, [own_f32, own_half, own_half, gain_row], (mid, gain_two, cotangent), d_hidden_two, "d_mid"
    )
    d_mid_own, act_later, d_up_later = lax.optimization_barrier((d_mid_own, act_later, d_up))
    d_mid_halves = all_blocks(d_mid_own, n)
    out_parts = project_sum(scal, [act_later], w_down, n, "project_down")
    grad_up = mm(d_up_later, hidden_two, TN).astype(BF16)
    d_mid_halves, out_parts, grad_up = lax.optimization_barrier((d_mid_halves, out_parts, grad_up))
    grad_up = scattered(grad_up, 1)
    out_sent, out_kept = sum_first(out_parts, n)
    d_mid_low, d_attended = project_back(scal, d_mid_halves, w_out, n)

    def sent_back(d_two, d_one, after=()):
        across = tied(swap(d_one, 1, "seq"), after)
        sent = (d_two.astype(F32) + jnp.where(odd, across.astype(F32), 0.0)).astype(BF16)
        return across, sent

    def back(g, d_attended):
        return attend_back(scal, g, query, segments[g], low, attended[g], d_attended, lse[g], cosine, sine, n)

    d_attended, out_sent = lax.optimization_barrier((d_attended, out_sent))
    out_terms = sum_second(out_sent, out_kept, n)
    dq, d_two, d_one, d_own = back(0, d_attended)
    low_later = tied(d_mid_low, dq)
    grad_out = jnp.concatenate([mm(a, low_later, TN).astype(BF16) for a in attended], axis=0)
    across, sent = sent_back(d_two, d_one, grad_out)
    grad_out = scattered(grad_out, 1)
    out_own = own_rows(output_kernel, scal, [own_half, own_half], (mid,), out_terms, "output")
    out_halves = all_blocks(out_own, n)
    d_attended, sent, across, out_own = lax.optimization_barrier((d_attended, sent, across, out_own))
    back_two = lax.ppermute(sent, "seq", left_two)
    dq_1, d_two_1, d_one_1, d_own_1 = back(1, d_attended)
    across_1, sent_1 = sent_back(d_two_1, d_one_1, back_two)
    sent_1, back_two = lax.optimization_barrier((sent_1, back_two))
    back_two_1 = lax.ppermute(sent_1, "seq", left_two)
    first = finish(scal, d_own, across, back_two, dq, cosine, sine, n)
    output = place(scal, out_halves, tuple(range(n)), BF16, n)
    back_two_1 = tied(back_two_1, (first, output, grad_down))
    second = finish(scal, d_own_1, across_1, back_two_1, dq_1, cosine, sine, n)
    d_gain_one, parts = project_one_back(scal, [first, second], (w_query, w_key, w_value), block_input, n)
    d_one_sent, d_one_kept = sum_first(parts, n)
    d_one_sent, first, second = lax.optimization_barrier((d_one_sent, first, second))
    d_hidden_one = sum_second(d_one_sent, d_one_kept, n)
    grad_first = mm(hidden_one, first, TN).astype(BF16)
    grad_second = mm(hidden_one, second, TN).astype(BF16)
    gains = seq_sums(jnp.concatenate([d_gain_one, d_gain_two], axis=0))
    d_hidden_one, gains = tied((d_hidden_one, gains), (grad_first, grad_second, grad_gate))
    grad_qkv = [scattered(grad_first, 0), scattered(grad_second, 0)]
    input_grad, *input_own_halves = own_rows(
        input_kernel, scal, [own_f32, own_half, own_half], (block_input, gain_one, d_mid), d_hidden_one, "input"
    )
    input_halves = all_blocks(input_own_halves, n)
    for bit in bits_of(n):
        gains = gains + swap(gains, bit)
    early, late = tuple(range(n - 1)), (n - 1,)
    early_halves = [side[: n - 1] for side in input_halves]
    grad_input = place(scal, tied(early_halves, grad_up), early, F32, n, own=input_grad)
    grad_input = place(scal, input_halves, late, F32, n, whole=grad_input)

    part = grad_qkv[0].shape[1] // 3
    grad_query, grad_key, grad_value = (
        jnp.concatenate([g[:, k * part : (k + 1) * part] for g in grad_qkv], axis=1).astype(F32)
        for k in range(3)
    )
    return (
        output, grad_input, gains[0], grad_query, grad_key, grad_value, grad_out.astype(F32), gains[1],
        grad_gate.T.astype(F32), grad_up.T.astype(F32), grad_down.astype(F32),
    )


def solution(mesh):
    in_specs = (
        P("seq", None), P(), P(None, "tp"), P(None, "tp"), P(None, "tp"), P("tp", None), P(),
        P(None, "tp"), P(None, "tp"), P("tp", None), P("seq"), P("seq", None),
    )
    out_specs = (
        P("seq", None), P("seq", None), P("seq"), P("seq", "tp"), P("seq", "tp"), P("seq", "tp"),
        P("tp", "seq"), P("seq"), P("seq", "tp"), P("seq", "tp"), P("tp", "seq"),
    )
    return jax.shard_map(
        on_device, mesh=mesh, in_specs=in_specs, out_specs=out_specs, check_vma=False
    )
```

```python
import jax
import jax.numpy as jnp
from jax import lax
from jax.experimental import pallas as pl
from jax.experimental.pallas import tpu as pltpu
from jax.sharding import PartitionSpec as P

HEAD = 128
WINDOW = 2048
LOG2E = 1.4426950408889634
SCALE = HEAD ** (-0.5)
NEG = -1e30
F32 = jnp.float32
BF16 = jnp.bfloat16
MIB = 1024 * 1024
STEPS = 4
GROUPS = 2

NN = (((1,), (0,)), ((), ()))
NT = (((1,), (1,)), ((), ()))
TN = (((0,), (0,)), ((), ()))


def mm(a, b, dims=NN):
    return lax.dot_general(a, b, dims, preferred_element_type=F32)


def tied(values, after):
    return lax.optimization_barrier((values, after))[0]


def call(body, grid, in_specs, out_specs, outs, args, name, scratch=(), vmem=48, into=(), weight=0):
    count = len(args)
    if into:
        inner = body
        body = lambda *refs: inner(*refs[:count], *refs[count + len(into) :])
    return pl.pallas_call(
        body,
        grid_spec=pltpu.PrefetchScalarGridSpec(
            num_scalar_prefetch=1,
            grid=grid,
            in_specs=list(in_specs) + [pl.BlockSpec(memory_space=pl.ANY)] * len(into),
            out_specs=out_specs,
            scratch_shapes=list(scratch),
        ),
        input_output_aliases={count + k: k for k in range(len(into))},
        out_shape=[jax.ShapeDtypeStruct(shape, kind) for shape, kind in outs],
        compiler_params=pltpu.CompilerParams(vmem_limit_bytes=vmem * MIB),
        cost_estimate=pl.CostEstimate(flops=weight, bytes_accessed=0, transcendentals=0),
        name=name,
    )(*args, *into)


def fixed(shape):
    return pl.BlockSpec(shape, lambda *_: (0,) * len(shape), pipeline_mode=pl.Buffered(1))


def to_relative(array, me, n):
    rows = array.shape[0] // n
    return jnp.concatenate(
        [lax.dynamic_slice_in_dim(array, (r ^ me) * rows, rows, 0) for r in range(n)], axis=0
    )


def swap(array, bit, axis="tp"):
    size = lax.axis_size(axis)
    return lax.ppermute(array, axis, [(i, i ^ bit) for i in range(size)])


def bits_of(n):
    return [1 << b for b in range(n.bit_length() - 1)]


def sum_first(parts, n):
    cut = lambda r, side: parts[2 * r + side]
    if n == 4:
        three_left, three_right = swap(cut(3, 0), 1), swap(cut(3, 1), 2)
        one_left, two_right = swap(cut(1, 0), 1), swap(cut(2, 1), 2)
        one_right = (cut(1, 1).astype(F32) + three_right.astype(F32)).astype(BF16)
        two_left = (cut(2, 0).astype(F32) + three_left.astype(F32)).astype(BF16)
        return (one_right, two_left), ([cut(0, 0), one_left], [cut(0, 1), two_right])
    sides = []
    rows = parts[0].shape[0]
    for side, order in enumerate((bits_of(n), bits_of(n)[::-1])):
        held = {r: cut(r, side) for r in range(n)}
        for bit in order:
            sent = [r for r in held if r & bit]
            got = swap(jnp.concatenate([held[r] for r in sent]).astype(BF16), bit)
            held = {
                r ^ bit: held[r ^ bit].astype(F32) + got[k * rows : (k + 1) * rows].astype(F32)
                for k, r in enumerate(sent)
            }
        sides.append(held[0])
    return tuple(sides), ([], [])


def sum_second(sent, kept, n):
    if n == 4:
        one_right, two_left = swap(sent[0], 1), swap(sent[1], 2)
        return kept[0] + [two_left], kept[1] + [one_right]
    return [sent[0]], [sent[1]]


def all_blocks(own, n):
    left, right = own
    if n == 4:
        one_right, two_left = swap(right, 1), swap(left, 2)
        one_left, two_right = swap(left, 1), swap(right, 2)
        three_left, three_right = swap(two_left, 1), swap(one_right, 2)
        return [left, one_left, two_left, three_left], [right, one_right, two_right, three_right]
    sides = []
    rows = left.shape[0]
    for side, order in enumerate((bits_of(n)[::-1], bits_of(n))):
        held = {0: own[side]}
        for bit in order:
            have = sorted(held)
            got = swap(jnp.concatenate([held[r] for r in have]), bit)
            for k, r in enumerate(have):
                held[r ^ bit] = got[k * rows : (k + 1) * rows]
        sides.append([held[r] for r in range(n)])
    return sides[0], sides[1]


def rotated(a, cosine, sine):
    return a * cosine + pltpu.roll(a, HEAD // 2, 1) * sine


def total(refs):
    out = refs[0][...].astype(F32)
    for ref in refs[1:]:
        out = out + ref[...].astype(F32)
    return out


def heads_of(width):
    return [slice(h * HEAD, (h + 1) * HEAD) for h in range(width // HEAD)]


def keys_kernel(me_ref, x_ref, gain_ref, wk_ref, wv_ref, cos_ref, sin_ref, h_ref, all_ref, *kv_refs):
    x = x_ref[...].astype(F32)
    factor = lax.rsqrt(jnp.mean(x * x, axis=-1, keepdims=True) + 1e-06)
    hidden = (x * factor * gain_ref[...]).astype(BF16)
    h_ref[...] = hidden
    cosine, sine = cos_ref[...], sin_ref[...]
    for g, kv_ref in enumerate(kv_refs):
        width = kv_ref.shape[2]
        cols = slice(g * width, (g + 1) * width)
        key = mm(hidden, wk_ref[:, cols])
        for cut in heads_of(width):
            kv_ref[0, :, cut] = rotated(key[:, cut], cosine, sine).astype(BF16)
        kv_ref[1] = mm(hidden, wv_ref[:, cols]).astype(BF16)
        all_ref[2 * g : 2 * g + 2] = kv_ref[...]


def project_keys(scal, x, gain, wk, wv, cosine, sine, n):
    tokens, width = x.shape
    local = wk.shape[1]
    rows, part = tokens // n, local // GROUPS
    mine = lambda r, m: (r, 0)
    return call(
        keys_kernel,
        (n,),
        [
            pl.BlockSpec((rows, width), lambda r, m: (r ^ m[0], 0)),
            fixed((1, width)),
            fixed((width, local)),
            fixed((width, local)),
            pl.BlockSpec((rows, HEAD), mine),
            pl.BlockSpec((rows, HEAD), mine),
        ],
        [pl.BlockSpec((rows, width), mine)]
        + [pl.BlockSpec((2 * GROUPS, rows, part), lambda r, m: (0, r, 0))]
        + [pl.BlockSpec((2, rows, part), lambda r, m: (0, r, 0))] * GROUPS,
        [((tokens, width), BF16), ((2 * GROUPS, tokens, part), BF16)] + [((2, tokens, part), BF16)] * GROUPS,
        (scal, x, gain, wk, wv, cosine, sine),
        "project_keys",
    )


def query_kernel(me_ref, h_ref, w_ref, cos_ref, sin_ref, q_ref):
    pre = mm(h_ref[...], w_ref[...])
    for cut in heads_of(pre.shape[1]):
        q_ref[:, cut] = rotated(pre[:, cut], cos_ref[...], sin_ref[...]).astype(BF16)


def project_query(scal, hidden, wq, cosine, sine, n):
    tokens, width = hidden.shape
    local = wq.shape[1]
    rows = tokens // n
    mine = lambda r, m: (r, 0)
    return call(
        query_kernel,
        (n,),
        [
            pl.BlockSpec((rows, width), mine),
            fixed((width, local)),
            pl.BlockSpec((rows, HEAD), mine),
            pl.BlockSpec((rows, HEAD), mine),
        ],
        [pl.BlockSpec((rows, local), mine)],
        [((tokens, local), BF16)],
        (scal, hidden, wq, cosine, sine),
        "project_query",
    )[0]


def act_kernel(me_ref, cot_ref, w_ref, rel_ref, d_ref):
    cot = cot_ref[...]
    rel_ref[...] = cot
    d_ref[...] = mm(cot, w_ref[...], NT)


def project_cotangent(scal, cot, w_down, n):
    tokens, width = cot.shape
    hid = w_down.shape[0]
    rows = tokens // n
    mine = lambda r, m: (r, 0)
    return call(
        act_kernel,
        (n,),
        [pl.BlockSpec((rows, width), lambda r, m: (r ^ m[0], 0)), fixed((hid, width))],
        [pl.BlockSpec((rows, width), mine), pl.BlockSpec((rows, hid), mine)],
        [((tokens, width), BF16), ((tokens, hid), F32)],
        (scal, cot, w_down),
        "project_cotangent",
    )


def masked(s, first, low, query_at, diagonal):
    key_at = first + lax.broadcasted_iota(jnp.int32, s.shape, 0)
    keep = key_at >= low
    if diagonal:
        keep = keep & (key_at <= query_at)
    return jnp.where(keep, s, NEG)


def lay_window(n, rows, me, odd, which, two_ref, odd_ref, even_ref, own_ref, put):
    for seg, refs in enumerate(((two_ref,), (odd_ref, even_ref), (own_ref,))):
        for sub in range(n):
            here = pl.ds(pl.multiple_of((sub ^ me) * rows, rows), rows)
            at = slice((seg * n + sub) * rows, (seg * n + sub + 1) * rows)
            if len(refs) == 1:
                put(at, refs[0][which, here, :])
            else:
                put(at, jnp.where(odd != 0, refs[0][which, here, :], refs[1][which, here, :]))


def lanes(array):
    return [array[:, j * HEAD : (j + 1) * HEAD] for j in range(array.shape[1] // HEAD)]


def attend_kernel(n, at, s_ref_, q_ref, two_ref, odd_ref, even_ref, own_ref, low_ref, o_ref, lse_ref, s_ref, k_ref, v_ref):
    rows = q_ref.shape[0]
    me, odd = s_ref_[0], s_ref_[1]
    start = ((pl.program_id(1) + at) ^ me) * rows
    chunks = 2 * n + 1

    @pl.when(pl.program_id(1) == 0)
    def _():
        def put_key(at, block):
            k_ref[at, :] = block

        def put_value(at, block):
            v_ref[at, :] = block

        window = (two_ref, odd_ref, even_ref, own_ref)
        lay_window(n, rows, me, odd, 0, *window, put_key)
        lay_window(n, rows, me, odd, 1, *window, put_value)

    q = q_ref[...]
    low = low_ref[...] - start
    low = jnp.concatenate([low] * (rows // HEAD), axis=1)
    key_at = lax.broadcasted_iota(jnp.int32, (rows, rows), 1)
    query_at = lax.broadcasted_iota(jnp.int32, (rows, rows), 0)
    top = jnp.full((rows, HEAD), NEG, F32)
    for c in range(chunks):
        here = pl.ds(pl.multiple_of(start + c * rows, rows), rows)
        s = mm(q, k_ref[here, :], NT)
        keep = key_at >= low - c * rows
        if c == chunks - 1:
            keep = keep & (key_at <= query_at)
        s = jnp.where(keep, s, NEG)
        s_ref[:, c * rows : (c + 1) * rows] = s
        for lane in lanes(s):
            top = jnp.maximum(top, lane)
    top = jnp.max(top, axis=1, keepdims=True) * (SCALE * LOG2E)
    whole = jnp.zeros((rows, HEAD), F32)
    acc = jnp.zeros((rows, HEAD), F32)
    for c in range(chunks):
        here = pl.ds(pl.multiple_of(start + c * rows, rows), rows)
        p = jnp.exp2(s_ref[:, c * rows : (c + 1) * rows] * (SCALE * LOG2E) - top)
        for lane in lanes(p):
            whole = whole + lane
        acc = acc + mm(p.astype(BF16), v_ref[here, :])
    whole = jnp.sum(whole, axis=1, keepdims=True)
    o_ref[...] = (acc / whole).astype(BF16)
    lse = jnp.broadcast_to(top + jnp.log2(whole), (rows, HEAD)).T
    lse_ref[...] = lse[:1, :].reshape(lse_ref.shape)


def attend(scal, g, q, segments, low, n, at, count, into=()):
    tokens = q.shape[0]
    part = segments[0].shape[2]
    heads, rows = part // HEAD, tokens // n
    pairs = heads * tokens * (2 * tokens + rows)
    segment = pl.BlockSpec((2, tokens, HEAD), lambda h, r, m: (0, 0, h))
    across = pl.BlockSpec((2, tokens, HEAD), lambda h, r, m: (g, 0, h))
    return call(
        lambda *refs: attend_kernel(n, at, *refs),
        (heads, count),
        [pl.BlockSpec((rows, HEAD), lambda h, r, m: (r + at, g * heads + h))]
        + [segment, across, segment, segment]
        + [pl.BlockSpec((rows, HEAD), lambda h, r, m: (r + at, 0))],
        [
            pl.BlockSpec((rows, HEAD), lambda h, r, m: (r + at, h)),
            pl.BlockSpec((1, 1, rows), lambda h, r, m: (h, 0, r + at)),
        ],
        [((tokens, part), BF16), ((heads, 1, tokens), F32)],
        (scal, q, *segments, low),
        "attend",
        scratch=[
            pltpu.VMEM((rows, (2 * n + 1) * rows), F32),
            pltpu.VMEM((3 * tokens, HEAD), BF16),
            pltpu.VMEM((3 * tokens, HEAD), BF16),
        ],
        into=into,
    )


def attend_back_kernel(
    n, s_ref_, q_ref, two_ref, odd_ref, even_ref, own_ref, low_ref, o_ref, do_ref, lse_ref, cos_ref, sin_ref,
    dq_ref, d_two_ref, d_one_ref, d_own_ref, dk_acc, dv_acc, k_ref, kt_ref, v_ref,
):
    rows = q_ref.shape[0]
    me, odd = s_ref_[0], s_ref_[1]
    r = pl.program_id(1)
    rb = r ^ me
    chunks = 2 * n + 1

    @pl.when(r == 0)
    def _():
        def put_key(at, block):
            k_ref[at, :] = block
            kt_ref[:, at] = block.T
            dk_acc[at, :] = jnp.zeros((rows, HEAD), F32)
            dv_acc[at, :] = jnp.zeros((rows, HEAD), F32)

        def put_value(at, block):
            v_ref[at, :] = block

        window = (two_ref, odd_ref, even_ref, own_ref)
        lay_window(n, rows, me, odd, 0, *window, put_key)
        lay_window(n, rows, me, odd, 1, *window, put_value)

    q, do = q_ref[...], do_ref[...]
    low = low_ref[...]
    lse = lse_ref[...].reshape(1, rows)
    delta = jnp.sum((do.astype(F32) * o_ref[...].astype(F32)).T, axis=0, keepdims=True)
    query_at = (rb + 2 * n) * rows + lax.broadcasted_iota(jnp.int32, (1, rows), 1)
    steps = []
    for c in range(chunks):
        first = pl.multiple_of((rb + c) * rows, rows)
        here = pl.ds(first, rows)
        s = mm(k_ref[here, :], q, NT) * (SCALE * LOG2E)
        s = masked(s, first, low, query_at, c == chunks - 1)
        p = jnp.exp2(s - lse)
        dp = mm(v_ref[here, :], do, NT)
        steps.append((here, p.astype(BF16), (p * (dp - delta)).astype(BF16)))
    dqt = jnp.zeros((HEAD, rows), F32)
    for here, p, ds in steps:
        dv_acc[here, :] += mm(p, do)
        dk_acc[here, :] += mm(ds, q)
        dqt = dqt + mm(kt_ref[:, here], ds)
    dq_ref[...] = rotated(dqt.T * SCALE, cos_ref[...], -sin_ref[...]).astype(BF16)

    @pl.when(r == n - 1)
    def _():
        for seg, out_ref in enumerate((d_two_ref, d_one_ref, d_own_ref)):
            for sub in range(n):
                here = pl.ds(pl.multiple_of((sub ^ me) * rows, rows), rows)
                at = slice((seg * n + sub) * rows, (seg * n + sub + 1) * rows)
                out_ref[0, here, :] = (dk_acc[at, :] * SCALE).astype(BF16)
                out_ref[1, here, :] = dv_acc[at, :].astype(BF16)


def attend_back(scal, g, q, segments, low, attended, d_attended, lse, cosine, sine, n):
    tokens = q.shape[0]
    part = segments[0].shape[2]
    heads, rows = part // HEAD, tokens // n
    pairs = heads * tokens * (2 * tokens + rows)
    block = pl.BlockSpec((rows, HEAD), lambda h, r, m: (r, h))
    shared = pl.BlockSpec((rows, HEAD), lambda h, r, m: (r, g * heads + h))
    segment = pl.BlockSpec((2, tokens, HEAD), lambda h, r, m: (0, 0, h))
    across = pl.BlockSpec((2, tokens, HEAD), lambda h, r, m: (g, 0, h))
    table = pl.BlockSpec((rows, HEAD), lambda h, r, m: (r, 0))
    return call(
        lambda *refs: attend_back_kernel(n, *refs),
        (heads, n),
        [shared]
        + [segment, across, segment, segment]
        + [
            pl.BlockSpec((1, rows), lambda h, r, m: (0, r)),
            block,
            shared,
            pl.BlockSpec((1, 1, rows), lambda h, r, m: (h, 0, r)),
            table,
            table,
        ],
        [block] + [segment] * 3,
        [((tokens, part), BF16)] + [((2, tokens, part), BF16)] * 3,
        (scal, q, *segments, low, attended, d_attended, lse, cosine, sine),
        "attend_back",
        weight=69_000_000_000,
        scratch=[
            pltpu.VMEM((3 * tokens, HEAD), F32),
            pltpu.VMEM((3 * tokens, HEAD), F32),
            pltpu.VMEM((3 * tokens, HEAD), BF16),
            pltpu.VMEM((HEAD, 3 * tokens), BF16),
            pltpu.VMEM((3 * tokens, HEAD), BF16),
        ],
    )


def put_part(value, refs):
    half = refs[0].shape[1]
    value = value.astype(BF16)
    for r in range(len(refs) // 2):

        @pl.when(pl.program_id(0) == r)
        def _():
            refs[2 * r][...] = value[:, :half]
            refs[2 * r + 1][...] = value[:, half:]


def part_outs(n, rows, width):
    half = (rows, width // 2)
    return [pl.BlockSpec(half, lambda *_: (0, 0))] * (2 * n), [(half, BF16)] * (2 * n)


def sum_kernel(count, me_ref, *refs):
    arrays, w_ref, part_refs = refs[:count], refs[count], refs[count + 1 :]
    deep = arrays[0].shape[1]
    acc = mm(arrays[0][...], w_ref[:deep, :])
    for g in range(1, count):
        acc = acc + mm(arrays[g][...], w_ref[g * deep : (g + 1) * deep, :])
    put_part(acc, part_refs)


def project_sum(scal, arrays, weight, n, name, at=0, count=None):
    tokens, deep = arrays[0].shape
    width = weight.shape[1]
    rows = tokens // n
    count = n if count is None else count
    specs, outs = part_outs(count, rows, width)
    return call(
        lambda *refs: sum_kernel(len(arrays), *refs),
        (count,),
        [pl.BlockSpec((rows, deep), lambda r, m: (r + at, 0))] * len(arrays) + [fixed(weight.shape)],
        specs,
        outs,
        (scal, *arrays, weight),
        name,
    )


def own_rows(kernel, scal, outs, args, lists, name):
    rows, half = lists[0][0].shape
    flat = tuple(lists[0]) + tuple(lists[1])
    count = len(args)

    def body(_, *refs):
        left = refs[count : count + len(lists[0])]
        right = refs[count + len(lists[0]) : count + len(flat)]
        summed = jnp.concatenate([total(left), total(right)], axis=1)
        kernel(summed, *refs[:count], *refs[count + len(flat) :])

    def spec(shape):
        if shape[0] == 1:
            return pl.BlockSpec(shape, lambda i, m: (0, 0))
        if shape[0] == rows:
            return pl.BlockSpec((rows // STEPS, shape[1]), lambda i, m: (i, 0))
        return pl.BlockSpec((rows // STEPS, shape[1]), lambda i, m: (m[0] * STEPS + i, 0))

    return call(
        body,
        (STEPS,),
        [spec(a.shape) for a in args] + [spec((rows, half))] * len(flat),
        [spec(shape) for shape, _ in outs],
        outs,
        (scal, *args, *flat),
        name,
    )


def mid_kernel(summed, x_ref, gain_ref, mid_ref, left_ref, right_ref):
    half = left_ref.shape[1]
    mid = x_ref[...].astype(F32) + summed
    mid_ref[...] = mid
    factor = lax.rsqrt(jnp.mean(mid * mid, axis=-1, keepdims=True) + 1e-06)
    hidden = (mid * factor * gain_ref[...]).astype(BF16)
    left_ref[...] = hidden[:, :half]
    right_ref[...] = hidden[:, half:]


def add_rows(out_ref, values):
    @pl.when(pl.program_id(0) == 0)
    def _():
        out_ref[...] = jnp.zeros_like(out_ref)

    out_ref[...] += jnp.sum(values, axis=0, keepdims=True)


def back_norm(d_hidden, values, gain, d_gain_ref=None):
    factor = lax.rsqrt(jnp.mean(values * values, axis=-1, keepdims=True) + 1e-06)
    normed = values * factor
    if d_gain_ref is not None:
        add_rows(d_gain_ref, d_hidden * normed)
    e = d_hidden * gain
    return factor * (e - normed * jnp.mean(e * normed, axis=-1, keepdims=True))


def d_mid_kernel(d_hidden, mid_ref, gain_ref, cot_ref, d_mid_ref, left_ref, right_ref, d_gain_ref):
    half = left_ref.shape[1]
    d_mid = cot_ref[...].astype(F32) + back_norm(d_hidden, mid_ref[...], gain_ref[...], d_gain_ref)
    d_mid_ref[...] = d_mid
    left_ref[...] = d_mid[:, :half].astype(BF16)
    right_ref[...] = d_mid[:, half:].astype(BF16)


def input_kernel(d_hidden, x_ref, gain_ref, d_mid_ref, own_ref, left_ref, right_ref):
    half = left_ref.shape[1]
    grad = d_mid_ref[...] + back_norm(d_hidden, x_ref[...].astype(F32), gain_ref[...])
    own_ref[...] = grad
    left_ref[...] = grad[:, :half].astype(BF16)
    right_ref[...] = grad[:, half:].astype(BF16)


def output_kernel(summed, mid_ref, left_ref, right_ref):
    half = left_ref.shape[1]
    out = (mid_ref[...] + summed).astype(BF16)
    left_ref[...] = out[:, :half]
    right_ref[...] = out[:, half:]


def lay_block(n, left_refs, right_refs, whole_ref):
    half = left_refs[0].shape[1]
    for r in range(n):

        @pl.when(pl.program_id(0) == r)
        def _():
            whole_ref[:, :half] = left_refs[r][...].astype(whole_ref.dtype)
            whole_ref[:, half:] = right_refs[r][...].astype(whole_ref.dtype)


def mlp_kernel(n, me_ref, *refs):
    left, right = refs[:n], refs[n : 2 * n]
    d_act_ref, wg_ref, wu_ref, h_ref, act_ref, dg_ref, du_ref = refs[2 * n : 2 * n + 7]
    lay_block(n, left, right, h_ref)
    hidden = h_ref[...]
    gate = mm(hidden, wg_ref[...], NT)
    up = mm(hidden, wu_ref[...], NT)
    d_act = d_act_ref[...]
    s = 1.0 / (1.0 + jnp.exp(-gate))
    silu = gate * s
    act_ref[...] = (silu * up).astype(BF16)
    d_gate = (d_act * up * s * (1.0 + gate * (1.0 - s))).astype(BF16)
    d_up = (d_act * silu).astype(BF16)
    dg_ref[...] = d_gate
    du_ref[...] = d_up
    put_part(mm(d_gate, wg_ref[...]) + mm(d_up, wu_ref[...]), refs[2 * n + 7 :])


def mlp(scal, halves, d_act, w_gate, w_up, n, at, count, into=()):
    left, right = (side[at : at + count] for side in halves)
    rows, half = left[0].shape
    hid, width = w_gate.shape
    tokens = rows * n
    mine = lambda r, m: (r + at, 0)
    specs, outs = part_outs(count, rows, width)
    results = call(
        lambda *refs: mlp_kernel(count, *refs),
        (count,),
        [fixed((rows, half))] * (2 * count)
        + [pl.BlockSpec((rows, hid), mine), fixed((hid, width)), fixed((hid, width))],
        [pl.BlockSpec((rows, width), mine)] + [pl.BlockSpec((rows, hid), mine)] * 3 + specs,
        [((tokens, width), BF16)] + [((tokens, hid), BF16)] * 3 + outs,
        (scal, *left, *right, d_act, w_gate, w_up),
        "mlp",
        vmem=56,
        into=into,
    )
    return results[:4], results[4:]


def outer_kernel(me_ref, *refs):
    *left, right_ref, out_ref = refs
    deep = left[0].shape[1]
    for g, ref in enumerate(left):
        out_ref[g * deep : (g + 1) * deep, :] = mm(ref[...], right_ref[...], TN).astype(BF16)


def outer(scal, left, right, name):
    tokens, deep = left[0].shape
    width = right.shape[1]
    steps = 4 if width % 512 == 0 else 3
    step = width // steps
    return call(
        outer_kernel,
        (steps,),
        [fixed((tokens, deep))] * len(left) + [pl.BlockSpec((tokens, step), lambda j, m: (0, j))],
        [pl.BlockSpec((len(left) * deep, step), lambda j, m: (0, j))],
        [((len(left) * deep, width), BF16)],
        (scal, *left, right),
        name,
    )[0]


def d_attended_kernel(n, me_ref, *refs):
    left, right = refs[:n], refs[n : 2 * n]
    w_ref, low_ref, d_ref = refs[2 * n :]
    lay_block(n, left, right, low_ref)
    d_ref[...] = mm(low_ref[...], w_ref[...], NT).astype(BF16)


def project_back(scal, halves, w_out, n):
    rows, half = halves[0][0].shape
    local, width = w_out.shape
    tokens = rows * n
    mine = lambda r, m: (r, 0)
    return call(
        lambda *refs: d_attended_kernel(n, *refs),
        (n,),
        [fixed((rows, half))] * (2 * n) + [fixed((local, width))],
        [pl.BlockSpec((rows, width), mine), pl.BlockSpec((rows, local), mine)],
        [((tokens, width), BF16), ((tokens, local), BF16)],
        (scal, *halves[0], *halves[1], w_out),
        "project_back",
    )


def place_kernel(blocks, has_own, me_ref, *refs):
    count = len(blocks)
    left, right, out_ref = refs[:count], refs[count : 2 * count], refs[-1]
    lay_block(count, left, right, out_ref)
    if has_own:

        @pl.when(pl.program_id(0) == 0)
        def _():
            out_ref[...] = refs[2 * count][...]


def place(scal, halves, blocks, kind, n, own=None, whole=None):
    rows, half = halves[0][0].shape
    first = blocks[0]
    arrays = [side[r] for side in halves for r in blocks]
    extra = [] if own is None else [own]
    held = [] if whole is None else [whole]
    return pl.pallas_call(
        lambda *refs: place_kernel(blocks, own is not None, *refs),
        grid_spec=pltpu.PrefetchScalarGridSpec(
            num_scalar_prefetch=1,
            grid=(len(blocks),),
            in_specs=[fixed((rows, half))] * len(arrays)
            + [fixed(e.shape) for e in extra]
            + [pl.BlockSpec(memory_space=pl.ANY)] * len(held),
            out_specs=pl.BlockSpec((rows, 2 * half), lambda r, m: ((r + first) ^ m[0], 0)),
        ),
        out_shape=jax.ShapeDtypeStruct((rows * n, 2 * half), kind),
        input_output_aliases={1 + len(arrays) + len(extra): 0} if held else {},
        compiler_params=pltpu.CompilerParams(vmem_limit_bytes=40 * MIB),
        cost_estimate=pl.CostEstimate(flops=0, bytes_accessed=0, transcendentals=0),
        name="place",
    )(scal, *arrays, *extra, *held)


def finish_kernel(s_ref_, own_ref, across_ref, back_ref, dq_ref, cos_ref, sin_ref, all_ref):
    part = dq_ref.shape[1]
    share = jnp.where(s_ref_[1] != 0, 0.0, 1.0)
    whole = own_ref[...].astype(F32) + back_ref[...].astype(F32) + across_ref[...].astype(F32) * share
    all_ref[:, :part] = dq_ref[...]
    for h, cut in enumerate(heads_of(part)):
        to = slice(part + h * HEAD, part + (h + 1) * HEAD)
        all_ref[:, to] = rotated(whole[0, :, cut], cos_ref[...], -sin_ref[...]).astype(BF16)
    all_ref[:, 2 * part :] = whole[1].astype(BF16)


def finish(scal, own, across, back, dq, cosine, sine, n):
    tokens, part = dq.shape
    rows = tokens // n
    segment = pl.BlockSpec((2, rows, part), lambda r, m: (0, r, 0))
    mine = lambda r, m: (r, 0)
    return call(
        finish_kernel,
        (n,),
        [segment] * 3
        + [pl.BlockSpec((rows, part), mine), pl.BlockSpec((rows, HEAD), mine), pl.BlockSpec((rows, HEAD), mine)],
        [pl.BlockSpec((rows, 3 * part), mine)],
        [((tokens, 3 * part), BF16)],
        (scal, own, across, back, dq, cosine, sine),
        "finish",
    )[0]


def d_one_kernel(me_ref, *refs):
    grads, weights = refs[:GROUPS], refs[GROUPS : GROUPS + 3]
    part = grads[0].shape[1] // 3
    acc = None
    for g, grad in enumerate(grads):
        for k, w_ref in enumerate(weights):
            term = mm(grad[:, k * part : (k + 1) * part], w_ref[:, g * part : (g + 1) * part], NT)
            acc = term if acc is None else acc + term
    put_part(acc, refs[GROUPS + 3 :])


def project_one_back(scal, grads, weights, n, at, count):
    tokens, triple = grads[0].shape
    width, local = weights[0].shape
    rows = tokens // n
    specs, outs = part_outs(count, rows, width)
    return call(
        d_one_kernel,
        (count,),
        [pl.BlockSpec((rows, triple), lambda r, m: (r + at, 0))] * GROUPS + [fixed((width, local))] * 3,
        specs,
        outs,
        (scal, *grads, *weights),
        "project_one_back",
    )


def gain_kernel(n, me_ref, x_ref, *refs):
    parts, gain_ref = refs[:-1], refs[-1]
    half = parts[0].shape[1]
    x = x_ref[...].astype(F32)
    normed = x * lax.rsqrt(jnp.mean(x * x, axis=-1, keepdims=True) + 1e-06)
    part = jnp.concatenate([parts[0][...], parts[1][...]], axis=1)
    for r in range(1, n):
        this = jnp.concatenate([parts[2 * r][...], parts[2 * r + 1][...]], axis=1)
        part = jnp.where(lax.div(pl.program_id(0), STEPS) == r, this, part)
    add_rows(gain_ref, part.astype(F32) * normed)


def gain_back(scal, x, parts, n):
    rows, half = parts[0].shape
    step = rows // STEPS
    return call(
        lambda *refs: gain_kernel(n, *refs),
        (n * STEPS,),
        [pl.BlockSpec((step, 2 * half), lambda i, m: ((lax.div(i, STEPS) ^ m[0]) * STEPS + lax.rem(i, STEPS), 0))]
        + [
            pl.BlockSpec((step, half), lambda i, m, r=k // 2: (jnp.clip(i - r * STEPS, 0, STEPS - 1), 0))
            for k in range(2 * n)
        ],
        [pl.BlockSpec((1, 2 * half), lambda i, m: (0, 0))],
        [((1, 2 * half), F32)],
        (scal, x, *parts),
        "gain_back",
    )[0]


def seq_sums(sums):
    peers = lax.axis_size("seq")
    at = lax.axis_index("seq")
    for bit in bits_of(peers)[::-1]:
        half = sums.shape[1] // 2
        upper = (at & bit) != 0
        low_part, high_part = sums[:, :half], sums[:, half:]
        kept = jnp.where(upper, high_part, low_part)
        sums = kept + swap(jnp.where(upper, low_part, high_part), bit, "seq")
    return sums


def scattered(grad, dim):
    return lax.psum_scatter(grad, "seq", scatter_dimension=dim, tiled=True)


def on_device(
    block_input, norm_one, w_query, w_key, w_value, w_out, norm_two, w_gate, w_up, w_down,
    starts, cotangent,
):
    tokens, width = block_input.shape
    hid = w_gate.shape[1]
    n = lax.axis_size("tp")
    me = lax.axis_index("tp")
    peers = lax.axis_size("seq")
    at = lax.axis_index("seq")
    rows = tokens // n
    odd = (at & 1) != 0
    scal = jnp.stack([me, at & 1]).astype(jnp.int32)
    gain_one, gain_two = norm_one[None, :], norm_two[None, :]

    order = to_relative(jnp.arange(tokens, dtype=jnp.int32), me, n)
    starts_here = to_relative(starts, me, n)
    positions = (at * tokens + order - starts_here).astype(F32)
    freqs = 10000.0 ** (-2.0 * jnp.arange(HEAD // 2, dtype=F32) / HEAD)
    angles = positions[:, None] * freqs[None, :]
    cosine, sine = jnp.cos(angles), jnp.sin(angles)
    cosine, sine = jnp.concatenate([cosine, cosine], 1), jnp.concatenate([-sine, sine], 1)
    low = jnp.maximum(starts_here - (at - 2) * tokens, order + 2 * tokens - WINDOW + 1)[None, :]

    low_wide = jnp.broadcast_to(low.reshape(tokens, 1), (tokens, HEAD))
    hidden_one, packed_all, *packed = project_keys(scal, block_input, gain_one, w_key, w_value, cosine, sine, n)

    right_two = [(i, i + 2) for i in range(peers - 2)]
    left_two = [(i + 2, i) for i in range(peers - 2)]
    to_odd = [(i, i + 1) for i in range(0, peers, 2)]
    to_even = [(i + 1, i) for i in range(0, peers, 2)]
    query = project_query(scal, hidden_one, w_query, cosine, sine, n)

    segments, attended, lse = [], [], []
    twos = [lax.ppermute(own, "seq", right_two) for own in packed]
    across_all = lax.ppermute(packed_all, "seq", to_odd)
    for g, own in enumerate(packed):
        two = tied(twos[g], attended[g - 1] if g else query)
        segments.append((two, across_all, lax.ppermute(two, "seq", to_even), own))
        if g < GROUPS - 1:
            out, peak = attend(scal, g, query, segments[g], low_wide, n, 0, n)
            attended.append(out)
            lse.append(peak)
    some = attend(scal, g, query, segments[g], low_wide, n, n - 1, 1)
    last_part = project_sum(scal, attended + [some[0]], w_out, n, "project_out", n - 1, 1)
    out, peak = attend(scal, g, query, segments[g], low_wide, n, 0, n - 1, into=tied(some, last_part))
    attended.append(out)
    lse.append(peak)
    parts = project_sum(scal, attended, w_out, n, "project_out", 0, n - 1)
    sent, kept = sum_first(list(parts) + list(last_part), n)
    sent, cot_later = lax.optimization_barrier((sent, cotangent))
    terms = sum_second(sent, kept, n)
    cot, d_act = project_cotangent(scal, cot_later, w_down, n)
    own_f32, own_half = ((rows, width), F32), ((rows, width // 2), BF16)
    mid, *hidden_own = own_rows(
        mid_kernel, scal, [own_f32, own_half, own_half], (block_input, gain_two), tied(terms, (cot, d_act)), "mid"
    )
    hidden_halves = all_blocks(hidden_own, n)
    weights = (w_gate.T, w_up.T)
    whole, own_part = mlp(scal, hidden_halves, d_act, *weights, n, 0, 1)
    whole, last_part = mlp(scal, hidden_halves, d_act, *weights, n, n - 1, 1, into=whole)
    whole, parts = mlp(scal, hidden_halves, d_act, *weights, n, 1, n - 2, into=tied(whole, last_part))
    hidden_two, activation, d_gate, d_up = whole
    parts = list(own_part) + list(parts) + list(last_part)

    d_two_sent, d_two_kept = sum_first(parts, n)
    d_two_sent, activation = lax.optimization_barrier((d_two_sent, activation))
    grad_down = outer(scal, [activation], cot, "grad_down")
    grad_down = scattered(grad_down, 1)
    d_hidden_two = sum_second(d_two_sent, d_two_kept, n)
    out_parts = project_sum(scal, [activation], w_down, n, "project_down")
    d_hidden_two = tied(d_hidden_two, out_parts)
    gain_row = ((1, width), F32)
    d_mid, *d_mid_own, d_gain_two = own_rows(
        d_mid_kernel, scal, [own_f32, own_half, own_half, gain_row], (mid, gain_two, cotangent), d_hidden_two, "d_mid"
    )
    d_mid_halves = all_blocks(d_mid_own, n)
    d_gate, d_up = tied((d_gate, d_up), (d_mid_halves[0][2], d_mid_halves[1][1]))
    grad_gate = outer(scal, [d_gate], hidden_two, "grad_gate")
    grad_up = outer(scal, [d_up], hidden_two, "grad_up")
    d_mid_halves = tied(d_mid_halves, (grad_gate, grad_up))
    grad_gate = scattered(grad_gate, 1)
    out_parts = tied(out_parts, d_mid_halves)
    out_sent, out_kept = sum_first(out_parts, n)
    d_mid_low, d_attended = project_back(scal, d_mid_halves, w_out, n)

    def sent_back(d_two, d_one):
        across = swap(d_one, 1, "seq")
        sent = (d_two.astype(F32) + jnp.where(odd, across.astype(F32), 0.0)).astype(BF16)
        return across, sent

    def back(g, d_attended):
        return attend_back(scal, g, query, segments[g], low, attended[g], d_attended, lse[g], cosine, sine, n)

    d_attended, out_sent = lax.optimization_barrier((d_attended, out_sent))
    out_terms = sum_second(out_sent, out_kept, n)
    grad_out = scattered(outer(scal, attended, d_mid_low, "grad_out"), 1)
    dq, d_two, d_one, d_own = back(0, d_attended)
    across, sent = sent_back(d_two, d_one)
    d_attended, sent, across = lax.optimization_barrier((d_attended, sent, across))
    back_two = lax.ppermute(sent, "seq", left_two)
    dq_1, d_two_1, d_one_1, d_own_1 = back(1, d_attended)
    d_one_1, back_two, out_terms = lax.optimization_barrier((d_one_1, back_two, out_terms))
    out_own = own_rows(output_kernel, scal, [own_half, own_half], (mid,), out_terms, "output")
    out_halves = all_blocks(out_own, n)
    across_1, sent_1 = sent_back(d_two_1, d_one_1)
    sent_1, across_1, back_two = lax.optimization_barrier((sent_1, across_1, back_two))
    back_two_1 = lax.ppermute(sent_1, "seq", left_two)
    back_two = tied(back_two, (out_halves[0][2], out_halves[1][1]))
    first = finish(scal, d_own, across, back_two, dq, cosine, sine, n)
    output = place(scal, out_halves, tuple(range(n)), BF16, n)
    back_two_1 = tied(back_two_1, output)
    grad_up = scattered(tied(grad_up, back_two_1), 1)
    second = finish(scal, d_own_1, across_1, back_two_1, dq_1, cosine, sine, n)
    weights = (w_query, w_key, w_value)
    last_part = project_one_back(scal, [first, second], weights, n, n - 1, 1)
    parts = project_one_back(scal, tied([first, second], last_part), weights, n, 0, n - 1)
    parts = list(parts) + list(last_part)
    d_one_sent, d_one_kept = sum_first(parts, n)
    grad_first = outer(scal, [hidden_one], tied(first, last_part), "grad_first")
    d_one_sent, parts, grad_first = lax.optimization_barrier((d_one_sent, parts, grad_first))
    d_hidden_one = sum_second(d_one_sent, d_one_kept, n)
    d_gain_one = gain_back(scal, block_input, parts, n)
    d_hidden_one = tied(d_hidden_one, d_gain_one)
    input_grad, *input_own_halves = own_rows(
        input_kernel, scal, [own_f32, own_half, own_half], (block_input, gain_one, d_mid), d_hidden_one, "input"
    )
    input_halves = all_blocks(input_own_halves, n)
    near = (input_halves[0][2], input_halves[1][1])
    second, gains = tied((second, jnp.concatenate([d_gain_one, d_gain_two], axis=0)), near)
    grad_second = outer(scal, [hidden_one], second, "grad_second")
    gains = seq_sums(gains)
    for bit in bits_of(n):
        gains = gains + swap(gains, bit)
    early, late = tuple(range(n - 1)), (n - 1,)
    early_halves = tied([side[: n - 1] for side in input_halves], (grad_first, grad_second))
    placed = place(scal, early_halves, early, F32, n, own=input_grad)
    grad_input = place(scal, input_halves, late, F32, n, whole=placed)
    grad_first, grad_second = scattered(grad_first, 0), scattered(grad_second, 0)

    grads, after = [], input_own_halves
    for grad in (grad_down, grad_gate, grad_out):
        after = tied(grad, after)
        grads.append(after)
    after = (after, placed)
    for grad in (grad_up, grad_first, grad_second):
        after = tied(grad, after)
        grads.append(after)
    grad_down, grad_gate, grad_out, grad_up, grad_first, grad_second = grads
    part = w_query.shape[1] // GROUPS
    grad_query, grad_key, grad_value = (
        jnp.concatenate([g[:, k * part : (k + 1) * part] for g in (grad_first, grad_second)], axis=1).astype(F32)
        for k in range(3)
    )
    return (
        output, grad_input, gains[0], grad_query, grad_key, grad_value, grad_out.astype(F32), gains[1],
        grad_gate.T.astype(F32), grad_up.T.astype(F32), grad_down.astype(F32),
    )


def solution(mesh):
    in_specs = (
        P("seq", None), P(), P(None, "tp"), P(None, "tp"), P(None, "tp"), P("tp", None), P(),
        P(None, "tp"), P(None, "tp"), P("tp", None), P("seq"), P("seq", None),
    )
    out_specs = (
        P("seq", None), P("seq", None), P("seq"), P("seq", "tp"), P("seq", "tp"), P("seq", "tp"),
        P("tp", "seq"), P("seq"), P("seq", "tp"), P("seq", "tp"), P("tp", "seq"),
    )
    return jax.shard_map(
        on_device, mesh=mesh, in_specs=in_specs, out_specs=out_specs, check_vma=False
    )
```

```python
import jax
import jax.numpy as jnp
from jax import lax
from jax.experimental import pallas as pl
from jax.experimental.pallas import tpu as pltpu
from jax.sharding import PartitionSpec as P

HEAD = 128
WINDOW = 2048
LOG2E = 1.4426950408889634
SCALE = HEAD ** (-0.5)
NEG = -1e30
F32 = jnp.float32
BF16 = jnp.bfloat16
MIB = 1024 * 1024
STEPS = 4
GROUPS = 2

NN = (((1,), (0,)), ((), ()))
NT = (((1,), (1,)), ((), ()))
TN = (((0,), (0,)), ((), ()))


def mm(a, b, dims=NN):
    return lax.dot_general(a, b, dims, preferred_element_type=F32)


def tied(values, after):
    return lax.optimization_barrier((values, after))[0]


def call(body, grid, in_specs, out_specs, outs, args, name, scratch=(), vmem=48, into=(), weight=0):
    count = len(args)
    if into:
        inner = body
        body = lambda *refs: inner(*refs[:count], *refs[count + len(into) :])
    return pl.pallas_call(
        body,
        grid_spec=pltpu.PrefetchScalarGridSpec(
            num_scalar_prefetch=1,
            grid=grid,
            in_specs=list(in_specs) + [pl.BlockSpec(memory_space=pl.ANY)] * len(into),
            out_specs=out_specs,
            scratch_shapes=list(scratch),
        ),
        input_output_aliases={count + k: k for k in range(len(into))},
        out_shape=[jax.ShapeDtypeStruct(shape, kind) for shape, kind in outs],
        compiler_params=pltpu.CompilerParams(vmem_limit_bytes=vmem * MIB),
        cost_estimate=pl.CostEstimate(flops=weight, bytes_accessed=0, transcendentals=0),
        name=name,
    )(*args, *into)


RESIDENT = pl.BlockSpec(memory_space=pltpu.VMEM)


def fixed(shape):
    return pl.BlockSpec(shape, lambda *_: (0,) * len(shape), pipeline_mode=pl.Buffered(1))


def to_relative(array, me, n):
    rows = array.shape[0] // n
    return jnp.concatenate(
        [lax.dynamic_slice_in_dim(array, (r ^ me) * rows, rows, 0) for r in range(n)], axis=0
    )


def swap(array, bit, axis="tp"):
    size = lax.axis_size(axis)
    return lax.ppermute(array, axis, [(i, i ^ bit) for i in range(size)])


def bits_of(n):
    return [1 << b for b in range(n.bit_length() - 1)]


def sum_first(parts, n):
    cut = lambda r, side: parts[2 * r + side]
    if n == 4:
        three_left, three_right = swap(cut(3, 0), 1), swap(cut(3, 1), 2)
        one_left, two_right = swap(cut(1, 0), 1), swap(cut(2, 1), 2)
        one_right = (cut(1, 1).astype(F32) + three_right.astype(F32)).astype(BF16)
        two_left = (cut(2, 0).astype(F32) + three_left.astype(F32)).astype(BF16)
        return (one_right, two_left), ([cut(0, 0), one_left], [cut(0, 1), two_right])
    sides = []
    rows = parts[0].shape[0]
    for side, order in enumerate((bits_of(n), bits_of(n)[::-1])):
        held = {r: cut(r, side) for r in range(n)}
        for bit in order:
            sent = [r for r in held if r & bit]
            got = swap(jnp.concatenate([held[r] for r in sent]).astype(BF16), bit)
            held = {
                r ^ bit: held[r ^ bit].astype(F32) + got[k * rows : (k + 1) * rows].astype(F32)
                for k, r in enumerate(sent)
            }
        sides.append(held[0])
    return tuple(sides), ([], [])


def sum_second(sent, kept, n):
    if n == 4:
        one_right, two_left = swap(sent[0], 1), swap(sent[1], 2)
        return kept[0] + [two_left], kept[1] + [one_right]
    return [sent[0]], [sent[1]]


def all_blocks(own, n):
    left, right = own
    if n == 4:
        one_right, two_left = swap(right, 1), swap(left, 2)
        one_left, two_right = swap(left, 1), swap(right, 2)
        three_left, three_right = swap(two_left, 1), swap(one_right, 2)
        return [left, one_left, two_left, three_left], [right, one_right, two_right, three_right]
    sides = []
    rows = left.shape[0]
    for side, order in enumerate((bits_of(n)[::-1], bits_of(n))):
        held = {0: own[side]}
        for bit in order:
            have = sorted(held)
            got = swap(jnp.concatenate([held[r] for r in have]), bit)
            for k, r in enumerate(have):
                held[r ^ bit] = got[k * rows : (k + 1) * rows]
        sides.append([held[r] for r in range(n)])
    return sides[0], sides[1]


def rotated(a, cosine, sine):
    return a * cosine + pltpu.roll(a, HEAD // 2, 1) * sine


def total(refs):
    out = refs[0][...].astype(F32)
    for ref in refs[1:]:
        out = out + ref[...].astype(F32)
    return out


def heads_of(width):
    return [slice(h * HEAD, (h + 1) * HEAD) for h in range(width // HEAD)]


def keys_kernel(me_ref, x_ref, gain_ref, wk_ref, wv_ref, cos_ref, sin_ref, h_ref, all_ref, *kv_refs):
    x = x_ref[...].astype(F32)
    factor = lax.rsqrt(jnp.mean(x * x, axis=-1, keepdims=True) + 1e-06)
    hidden = (x * factor * gain_ref[...]).astype(BF16)
    h_ref[...] = hidden
    cosine, sine = cos_ref[...], sin_ref[...]
    for g, kv_ref in enumerate(kv_refs):
        width = kv_ref.shape[2]
        cols = slice(g * width, (g + 1) * width)
        key = mm(hidden, wk_ref[:, cols])
        for cut in heads_of(width):
            kv_ref[0, :, cut] = rotated(key[:, cut], cosine, sine).astype(BF16)
        kv_ref[1] = mm(hidden, wv_ref[:, cols]).astype(BF16)
        all_ref[2 * g : 2 * g + 2] = kv_ref[...]


def project_keys(scal, x, gain, wk, wv, cosine, sine, n):
    tokens, width = x.shape
    local = wk.shape[1]
    rows, part = tokens // n, local // GROUPS
    mine = lambda r, m: (r, 0)
    return call(
        keys_kernel,
        (n,),
        [
            pl.BlockSpec((rows, width), lambda r, m: (r ^ m[0], 0)),
            fixed((1, width)),
            fixed((width, local)),
            fixed((width, local)),
            pl.BlockSpec((rows, HEAD), mine),
            pl.BlockSpec((rows, HEAD), mine),
        ],
        [pl.BlockSpec((rows, width), mine)]
        + [pl.BlockSpec((2 * GROUPS, rows, part), lambda r, m: (0, r, 0))]
        + [pl.BlockSpec((2, rows, part), lambda r, m: (0, r, 0))] * GROUPS,
        [((tokens, width), BF16), ((2 * GROUPS, tokens, part), BF16)] + [((2, tokens, part), BF16)] * GROUPS,
        (scal, x, gain, wk, wv, cosine, sine),
        "project_keys",
    )


def query_kernel(me_ref, h_ref, w_ref, cos_ref, sin_ref, q_ref):
    pre = mm(h_ref[...], w_ref[...])
    for cut in heads_of(pre.shape[1]):
        q_ref[:, cut] = rotated(pre[:, cut], cos_ref[...], sin_ref[...]).astype(BF16)


def project_query(scal, hidden, wq, cosine, sine, n):
    tokens, width = hidden.shape
    local = wq.shape[1]
    rows = tokens // n
    mine = lambda r, m: (r, 0)
    return call(
        query_kernel,
        (n,),
        [
            pl.BlockSpec((rows, width), mine),
            fixed((width, local)),
            pl.BlockSpec((rows, HEAD), mine),
            pl.BlockSpec((rows, HEAD), mine),
        ],
        [pl.BlockSpec((rows, local), mine)],
        [((tokens, local), BF16)],
        (scal, hidden, wq, cosine, sine),
        "project_query",
    )[0]


def act_kernel(me_ref, cot_ref, w_ref, rel_ref, d_ref):
    cot = cot_ref[...]
    rel_ref[...] = cot
    d_ref[...] = mm(cot, w_ref[...], NT)


def project_cotangent(scal, cot, w_down, n):
    tokens, width = cot.shape
    hid = w_down.shape[0]
    rows = tokens // n
    mine = lambda r, m: (r, 0)
    return call(
        act_kernel,
        (n,),
        [pl.BlockSpec((rows, width), lambda r, m: (r ^ m[0], 0)), fixed((hid, width))],
        [pl.BlockSpec((rows, width), mine), pl.BlockSpec((rows, hid), mine)],
        [((tokens, width), BF16), ((tokens, hid), F32)],
        (scal, cot, w_down),
        "project_cotangent",
    )


def masked(s, first, low, query_at, diagonal):
    key_at = first + lax.broadcasted_iota(jnp.int32, s.shape, 0)
    keep = key_at >= low
    if diagonal:
        keep = keep & (key_at <= query_at)
    return jnp.where(keep, s, NEG)


def lay_window(n, rows, me, odd, which, two_ref, odd_ref, even_ref, own_ref, put):
    for seg, refs in enumerate(((two_ref,), (odd_ref, even_ref), (own_ref,))):
        for sub in range(n):
            here = pl.ds(pl.multiple_of((sub ^ me) * rows, rows), rows)
            at = slice((seg * n + sub) * rows, (seg * n + sub + 1) * rows)
            if len(refs) == 1:
                put(at, refs[0][which, here, :])
            else:
                put(at, jnp.where(odd != 0, refs[0][which, here, :], refs[1][which, here, :]))


def lanes(array):
    return [array[:, j * HEAD : (j + 1) * HEAD] for j in range(array.shape[1] // HEAD)]


def attend_kernel(n, at, s_ref_, q_ref, two_ref, odd_ref, even_ref, own_ref, low_ref, o_ref, lse_ref, s_ref, k_ref, v_ref):
    rows = q_ref.shape[0]
    me, odd = s_ref_[0], s_ref_[1]
    start = ((pl.program_id(1) + at) ^ me) * rows
    chunks = 2 * n + 1

    @pl.when(pl.program_id(1) == 0)
    def _():
        def put_key(at, block):
            k_ref[at, :] = block

        def put_value(at, block):
            v_ref[at, :] = block

        window = (two_ref, odd_ref, even_ref, own_ref)
        lay_window(n, rows, me, odd, 0, *window, put_key)
        lay_window(n, rows, me, odd, 1, *window, put_value)

    q = q_ref[...]
    low = low_ref[...] - start
    low = jnp.concatenate([low] * (rows // HEAD), axis=1)
    key_at = lax.broadcasted_iota(jnp.int32, (rows, rows), 1)
    query_at = lax.broadcasted_iota(jnp.int32, (rows, rows), 0)
    top = jnp.full((rows, HEAD), NEG, F32)
    for c in range(chunks):
        here = pl.ds(pl.multiple_of(start + c * rows, rows), rows)
        s = mm(q, k_ref[here, :], NT)
        keep = key_at >= low - c * rows
        if c == chunks - 1:
            keep = keep & (key_at <= query_at)
        s = jnp.where(keep, s, NEG)
        s_ref[:, c * rows : (c + 1) * rows] = s
        for lane in lanes(s):
            top = jnp.maximum(top, lane)
    top = jnp.max(top, axis=1, keepdims=True) * (SCALE * LOG2E)
    whole = jnp.zeros((rows, HEAD), F32)
    acc = jnp.zeros((rows, HEAD), F32)
    for c in range(chunks):
        here = pl.ds(pl.multiple_of(start + c * rows, rows), rows)
        p = jnp.exp2(s_ref[:, c * rows : (c + 1) * rows] * (SCALE * LOG2E) - top)
        for lane in lanes(p):
            whole = whole + lane
        acc = acc + mm(p.astype(BF16), v_ref[here, :])
    whole = jnp.sum(whole, axis=1, keepdims=True)
    o_ref[...] = (acc / whole).astype(BF16)
    lse = jnp.broadcast_to(top + jnp.log2(whole), (rows, HEAD)).T
    lse_ref[...] = lse[:1, :].reshape(lse_ref.shape)


def attend(scal, g, q, segments, low, n, at, count, into=()):
    tokens = q.shape[0]
    part = segments[0].shape[2]
    heads, rows = part // HEAD, tokens // n
    pairs = heads * tokens * (2 * tokens + rows)
    segment = pl.BlockSpec((2, tokens, HEAD), lambda h, r, m: (0, 0, h))
    across = pl.BlockSpec((2, tokens, HEAD), lambda h, r, m: (g, 0, h))
    return call(
        lambda *refs: attend_kernel(n, at, *refs),
        (heads, count),
        [pl.BlockSpec((rows, HEAD), lambda h, r, m: (r + at, g * heads + h))]
        + [segment, across, segment, segment]
        + [pl.BlockSpec((rows, HEAD), lambda h, r, m: (r + at, 0))],
        [
            pl.BlockSpec((rows, HEAD), lambda h, r, m: (r + at, h)),
            pl.BlockSpec((1, 1, rows), lambda h, r, m: (h, 0, r + at)),
        ],
        [((tokens, part), BF16), ((heads, 1, tokens), F32)],
        (scal, q, *segments, low),
        "attend",
        scratch=[
            pltpu.VMEM((rows, (2 * n + 1) * rows), F32),
            pltpu.VMEM((3 * tokens, HEAD), BF16),
            pltpu.VMEM((3 * tokens, HEAD), BF16),
        ],
        into=into,
    )


def attend_back_kernel(
    n, s_ref_, q_ref, two_ref, odd_ref, even_ref, own_ref, low_ref, o_ref, do_ref, lse_ref, cos_ref, sin_ref,
    dq_ref, d_two_ref, d_one_ref, d_own_ref, dk_acc, dv_acc, k_ref, kt_ref, v_ref,
):
    rows = q_ref.shape[0]
    me, odd = s_ref_[0], s_ref_[1]
    r = pl.program_id(1)
    rb = r ^ me
    chunks = 2 * n + 1

    @pl.when(r == 0)
    def _():
        def put_key(at, block):
            k_ref[at, :] = block
            kt_ref[:, at] = block.T
            dk_acc[at, :] = jnp.zeros((rows, HEAD), F32)
            dv_acc[at, :] = jnp.zeros((rows, HEAD), F32)

        def put_value(at, block):
            v_ref[at, :] = block

        window = (two_ref, odd_ref, even_ref, own_ref)
        lay_window(n, rows, me, odd, 0, *window, put_key)
        lay_window(n, rows, me, odd, 1, *window, put_value)

    q, do = q_ref[...], do_ref[...]
    low = low_ref[...]
    lse = lse_ref[...].reshape(1, rows)
    delta = jnp.sum((do.astype(F32) * o_ref[...].astype(F32)).T, axis=0, keepdims=True)
    query_at = (rb + 2 * n) * rows + lax.broadcasted_iota(jnp.int32, (1, rows), 1)
    steps = []
    for c in range(chunks):
        first = pl.multiple_of((rb + c) * rows, rows)
        here = pl.ds(first, rows)
        s = mm(k_ref[here, :], q, NT) * (SCALE * LOG2E)
        s = masked(s, first, low, query_at, c == chunks - 1)
        p = jnp.exp2(s - lse)
        dp = mm(v_ref[here, :], do, NT)
        steps.append((here, p.astype(BF16), (p * (dp - delta)).astype(BF16)))
    dqt = jnp.zeros((HEAD, rows), F32)
    for here, p, ds in steps:
        dv_acc[here, :] += mm(p, do)
        dk_acc[here, :] += mm(ds, q)
        dqt = dqt + mm(kt_ref[:, here], ds)
    dq_ref[...] = rotated(dqt.T * SCALE, cos_ref[...], -sin_ref[...]).astype(BF16)

    @pl.when(r == n - 1)
    def _():
        for seg, out_ref in enumerate((d_two_ref, d_one_ref, d_own_ref)):
            for sub in range(n):
                here = pl.ds(pl.multiple_of((sub ^ me) * rows, rows), rows)
                at = slice((seg * n + sub) * rows, (seg * n + sub + 1) * rows)
                out_ref[0, here, :] = (dk_acc[at, :] * SCALE).astype(BF16)
                out_ref[1, here, :] = dv_acc[at, :].astype(BF16)


def attend_back(scal, g, q, segments, low, attended, d_attended, lse, cosine, sine, n):
    tokens = q.shape[0]
    part = segments[0].shape[2]
    heads, rows = part // HEAD, tokens // n
    pairs = heads * tokens * (2 * tokens + rows)
    block = pl.BlockSpec((rows, HEAD), lambda h, r, m: (r, h))
    shared = pl.BlockSpec((rows, HEAD), lambda h, r, m: (r, g * heads + h))
    segment = pl.BlockSpec((2, tokens, HEAD), lambda h, r, m: (0, 0, h))
    across = pl.BlockSpec((2, tokens, HEAD), lambda h, r, m: (g, 0, h))
    table = pl.BlockSpec((rows, HEAD), lambda h, r, m: (r, 0))
    return call(
        lambda *refs: attend_back_kernel(n, *refs),
        (heads, n),
        [shared]
        + [segment, across, segment, segment]
        + [
            pl.BlockSpec((1, rows), lambda h, r, m: (0, r)),
            block,
            shared,
            pl.BlockSpec((1, 1, rows), lambda h, r, m: (h, 0, r)),
            table,
            table,
        ],
        [block] + [segment] * 3,
        [((tokens, part), BF16)] + [((2, tokens, part), BF16)] * 3,
        (scal, q, *segments, low, attended, d_attended, lse, cosine, sine),
        "attend_back",
        weight=69_000_000_000,
        scratch=[
            pltpu.VMEM((3 * tokens, HEAD), F32),
            pltpu.VMEM((3 * tokens, HEAD), F32),
            pltpu.VMEM((3 * tokens, HEAD), BF16),
            pltpu.VMEM((HEAD, 3 * tokens), BF16),
            pltpu.VMEM((3 * tokens, HEAD), BF16),
        ],
    )


def put_part(value, refs):
    half = refs[0].shape[1]
    value = value.astype(BF16)
    for r in range(len(refs) // 2):

        @pl.when(pl.program_id(0) == r)
        def _():
            refs[2 * r][...] = value[:, :half]
            refs[2 * r + 1][...] = value[:, half:]


def part_outs(n, rows, width):
    half = (rows, width // 2)
    return [pl.BlockSpec(half, lambda *_: (0, 0))] * (2 * n), [(half, BF16)] * (2 * n)


def sum_kernel(count, me_ref, *refs):
    arrays, w_ref, part_refs = refs[:count], refs[count], refs[count + 1 :]
    deep = arrays[0].shape[1]
    acc = mm(arrays[0][...], w_ref[:deep, :])
    for g in range(1, count):
        acc = acc + mm(arrays[g][...], w_ref[g * deep : (g + 1) * deep, :])
    put_part(acc, part_refs)


def project_sum(scal, arrays, weight, n, name, at=0, count=None):
    tokens, deep = arrays[0].shape
    width = weight.shape[1]
    rows = tokens // n
    count = n if count is None else count
    specs, outs = part_outs(count, rows, width)
    return call(
        lambda *refs: sum_kernel(len(arrays), *refs),
        (count,),
        [pl.BlockSpec((rows, deep), lambda r, m: (r + at, 0))] * len(arrays) + [fixed(weight.shape)],
        specs,
        outs,
        (scal, *arrays, weight),
        name,
    )


def own_rows(kernel, scal, outs, args, lists, name):
    rows, half = lists[0][0].shape
    flat = tuple(lists[0]) + tuple(lists[1])
    count = len(args)

    def body(_, *refs):
        left = refs[count : count + len(lists[0])]
        right = refs[count + len(lists[0]) : count + len(flat)]
        summed = jnp.concatenate([total(left), total(right)], axis=1)
        kernel(summed, *refs[:count], *refs[count + len(flat) :])

    def spec(shape):
        if shape[0] == 1:
            return pl.BlockSpec(shape, lambda i, m: (0, 0))
        if shape[0] == rows:
            return pl.BlockSpec((rows // STEPS, shape[1]), lambda i, m: (i, 0))
        return pl.BlockSpec((rows // STEPS, shape[1]), lambda i, m: (m[0] * STEPS + i, 0))

    return call(
        body,
        (STEPS,),
        [spec(a.shape) for a in args] + [spec((rows, half))] * len(flat),
        [spec(shape) for shape, _ in outs],
        outs,
        (scal, *args, *flat),
        name,
    )


def mid_kernel(summed, x_ref, gain_ref, mid_ref, left_ref, right_ref):
    half = left_ref.shape[1]
    mid = x_ref[...].astype(F32) + summed
    mid_ref[...] = mid
    factor = lax.rsqrt(jnp.mean(mid * mid, axis=-1, keepdims=True) + 1e-06)
    hidden = (mid * factor * gain_ref[...]).astype(BF16)
    left_ref[...] = hidden[:, :half]
    right_ref[...] = hidden[:, half:]


def add_rows(out_ref, values):
    @pl.when(pl.program_id(0) == 0)
    def _():
        out_ref[...] = jnp.zeros_like(out_ref)

    out_ref[...] += jnp.sum(values, axis=0, keepdims=True)


def back_norm(d_hidden, values, gain, d_gain_ref=None):
    factor = lax.rsqrt(jnp.mean(values * values, axis=-1, keepdims=True) + 1e-06)
    normed = values * factor
    if d_gain_ref is not None:
        add_rows(d_gain_ref, d_hidden * normed)
    e = d_hidden * gain
    return factor * (e - normed * jnp.mean(e * normed, axis=-1, keepdims=True))


def d_mid_kernel(d_hidden, mid_ref, gain_ref, cot_ref, d_mid_ref, left_ref, right_ref, d_gain_ref):
    half = left_ref.shape[1]
    d_mid = cot_ref[...].astype(F32) + back_norm(d_hidden, mid_ref[...], gain_ref[...], d_gain_ref)
    d_mid_ref[...] = d_mid
    left_ref[...] = d_mid[:, :half].astype(BF16)
    right_ref[...] = d_mid[:, half:].astype(BF16)


def input_kernel(d_hidden, x_ref, gain_ref, d_mid_ref, own_ref, left_ref, right_ref):
    half = left_ref.shape[1]
    grad = d_mid_ref[...] + back_norm(d_hidden, x_ref[...].astype(F32), gain_ref[...])
    own_ref[...] = grad
    left_ref[...] = grad[:, :half].astype(BF16)
    right_ref[...] = grad[:, half:].astype(BF16)


def output_kernel(summed, mid_ref, left_ref, right_ref):
    half = left_ref.shape[1]
    out = (mid_ref[...] + summed).astype(BF16)
    left_ref[...] = out[:, :half]
    right_ref[...] = out[:, half:]


def lay_block(n, left_refs, right_refs, whole_ref):
    half = left_refs[0].shape[1]
    for r in range(n):

        @pl.when(pl.program_id(0) == r)
        def _():
            whole_ref[:, :half] = left_refs[r][...].astype(whole_ref.dtype)
            whole_ref[:, half:] = right_refs[r][...].astype(whole_ref.dtype)


def mlp_kernel(n, me_ref, *refs):
    left, right = refs[:n], refs[n : 2 * n]
    d_act_ref, wg_ref, wu_ref, h_ref, act_ref, dg_ref, du_ref = refs[2 * n : 2 * n + 7]
    lay_block(n, left, right, h_ref)
    hidden = h_ref[...]
    gate = mm(hidden, wg_ref[...], NT)
    up = mm(hidden, wu_ref[...], NT)
    d_act = d_act_ref[...]
    s = 1.0 / (1.0 + jnp.exp(-gate))
    silu = gate * s
    act_ref[...] = (silu * up).astype(BF16)
    d_gate = (d_act * up * s * (1.0 + gate * (1.0 - s))).astype(BF16)
    d_up = (d_act * silu).astype(BF16)
    dg_ref[...] = d_gate
    du_ref[...] = d_up
    put_part(mm(d_gate, wg_ref[...]) + mm(d_up, wu_ref[...]), refs[2 * n + 7 :])


def mlp(scal, halves, d_act, w_gate, w_up, n, at, count, into=()):
    left, right = (side[at : at + count] for side in halves)
    rows, half = left[0].shape
    hid, width = w_gate.shape
    tokens = rows * n
    mine = lambda r, m: (r + at, 0)
    specs, outs = part_outs(count, rows, width)
    results = call(
        lambda *refs: mlp_kernel(count, *refs),
        (count,),
        [fixed((rows, half))] * (2 * count)
        + [pl.BlockSpec((rows, hid), mine), RESIDENT, RESIDENT],
        [pl.BlockSpec((rows, width), mine)] + [pl.BlockSpec((rows, hid), mine)] * 3 + specs,
        [((tokens, width), BF16)] + [((tokens, hid), BF16)] * 3 + outs,
        (scal, *left, *right, d_act, w_gate, w_up),
        "mlp",
        vmem=34,
        into=into,
    )
    return results[:4], results[4:]


def outer_kernel(me_ref, *refs):
    *left, right_ref, out_ref = refs
    deep = left[0].shape[1]
    for g, ref in enumerate(left):
        out_ref[g * deep : (g + 1) * deep, :] = mm(ref[...], right_ref[...], TN).astype(BF16)


def outer(scal, left, right, name):
    tokens, deep = left[0].shape
    width = right.shape[1]
    steps = 4 if width % 512 == 0 else 3
    step = width // steps
    return call(
        outer_kernel,
        (steps,),
        [fixed((tokens, deep))] * len(left) + [pl.BlockSpec((tokens, step), lambda j, m: (0, j))],
        [pl.BlockSpec((len(left) * deep, step), lambda j, m: (0, j))],
        [((len(left) * deep, width), BF16)],
        (scal, *left, right),
        name,
    )[0]


def d_attended_kernel(n, me_ref, *refs):
    left, right = refs[:n], refs[n : 2 * n]
    w_ref, low_ref, d_ref = refs[2 * n :]
    lay_block(n, left, right, low_ref)
    d_ref[...] = mm(low_ref[...], w_ref[...], NT).astype(BF16)


def project_back(scal, halves, w_out, n):
    rows, half = halves[0][0].shape
    local, width = w_out.shape
    tokens = rows * n
    mine = lambda r, m: (r, 0)
    return call(
        lambda *refs: d_attended_kernel(n, *refs),
        (n,),
        [fixed((rows, half))] * (2 * n) + [fixed((local, width))],
        [pl.BlockSpec((rows, width), mine), pl.BlockSpec((rows, local), mine)],
        [((tokens, width), BF16), ((tokens, local), BF16)],
        (scal, *halves[0], *halves[1], w_out),
        "project_back",
    )


def place_kernel(blocks, has_own, me_ref, *refs):
    count = len(blocks)
    left, right, out_ref = refs[:count], refs[count : 2 * count], refs[-1]
    lay_block(count, left, right, out_ref)
    if has_own:

        @pl.when(pl.program_id(0) == 0)
        def _():
            out_ref[...] = refs[2 * count][...]


def place(scal, halves, blocks, kind, n, own=None, whole=None):
    rows, half = halves[0][0].shape
    first = blocks[0]
    arrays = [side[r] for side in halves for r in blocks]
    extra = [] if own is None else [own]
    held = [] if whole is None else [whole]
    return pl.pallas_call(
        lambda *refs: place_kernel(blocks, own is not None, *refs),
        grid_spec=pltpu.PrefetchScalarGridSpec(
            num_scalar_prefetch=1,
            grid=(len(blocks),),
            in_specs=[fixed((rows, half))] * len(arrays)
            + [fixed(e.shape) for e in extra]
            + [pl.BlockSpec(memory_space=pl.ANY)] * len(held),
            out_specs=pl.BlockSpec((rows, 2 * half), lambda r, m: ((r + first) ^ m[0], 0)),
        ),
        out_shape=jax.ShapeDtypeStruct((rows * n, 2 * half), kind),
        input_output_aliases={1 + len(arrays) + len(extra): 0} if held else {},
        compiler_params=pltpu.CompilerParams(vmem_limit_bytes=40 * MIB),
        cost_estimate=pl.CostEstimate(flops=0, bytes_accessed=0, transcendentals=0),
        name="place",
    )(scal, *arrays, *extra, *held)


def finish_kernel(s_ref_, own_ref, across_ref, back_ref, dq_ref, cos_ref, sin_ref, all_ref):
    part = dq_ref.shape[1]
    share = jnp.where(s_ref_[1] != 0, 0.0, 1.0)
    whole = own_ref[...].astype(F32) + back_ref[...].astype(F32) + across_ref[...].astype(F32) * share
    all_ref[:, :part] = dq_ref[...]
    for h, cut in enumerate(heads_of(part)):
        to = slice(part + h * HEAD, part + (h + 1) * HEAD)
        all_ref[:, to] = rotated(whole[0, :, cut], cos_ref[...], -sin_ref[...]).astype(BF16)
    all_ref[:, 2 * part :] = whole[1].astype(BF16)


def finish(scal, own, across, back, dq, cosine, sine, n):
    tokens, part = dq.shape
    rows = tokens // n
    segment = pl.BlockSpec((2, rows, part), lambda r, m: (0, r, 0))
    mine = lambda r, m: (r, 0)
    return call(
        finish_kernel,
        (n,),
        [segment] * 3
        + [pl.BlockSpec((rows, part), mine), pl.BlockSpec((rows, HEAD), mine), pl.BlockSpec((rows, HEAD), mine)],
        [pl.BlockSpec((rows, 3 * part), mine)],
        [((tokens, 3 * part), BF16)],
        (scal, own, across, back, dq, cosine, sine),
        "finish",
    )[0]


def d_one_kernel(me_ref, *refs):
    grads, weights = refs[:GROUPS], refs[GROUPS : GROUPS + 3]
    part = grads[0].shape[1] // 3
    acc = None
    for g, grad in enumerate(grads):
        for k, w_ref in enumerate(weights):
            term = mm(grad[:, k * part : (k + 1) * part], w_ref[:, g * part : (g + 1) * part], NT)
            acc = term if acc is None else acc + term
    put_part(acc, refs[GROUPS + 3 :])


def project_one_back(scal, grads, weights, n, at, count):
    tokens, triple = grads[0].shape
    width, local = weights[0].shape
    rows = tokens // n
    specs, outs = part_outs(count, rows, width)
    return call(
        d_one_kernel,
        (count,),
        [pl.BlockSpec((rows, triple), lambda r, m: (r + at, 0))] * GROUPS + [fixed((width, local))] * 3,
        specs,
        outs,
        (scal, *grads, *weights),
        "project_one_back",
    )


def gain_kernel(n, me_ref, x_ref, *refs):
    parts, gain_ref = refs[:-1], refs[-1]
    half = parts[0].shape[1]
    x = x_ref[...].astype(F32)
    normed = x * lax.rsqrt(jnp.mean(x * x, axis=-1, keepdims=True) + 1e-06)
    part = jnp.concatenate([parts[0][...], parts[1][...]], axis=1)
    for r in range(1, n):
        this = jnp.concatenate([parts[2 * r][...], parts[2 * r + 1][...]], axis=1)
        part = jnp.where(lax.div(pl.program_id(0), STEPS) == r, this, part)
    add_rows(gain_ref, part.astype(F32) * normed)


def gain_back(scal, x, parts, n):
    rows, half = parts[0].shape
    step = rows // STEPS
    return call(
        lambda *refs: gain_kernel(n, *refs),
        (n * STEPS,),
        [pl.BlockSpec((step, 2 * half), lambda i, m: ((lax.div(i, STEPS) ^ m[0]) * STEPS + lax.rem(i, STEPS), 0))]
        + [
            pl.BlockSpec((step, half), lambda i, m, r=k // 2: (jnp.clip(i - r * STEPS, 0, STEPS - 1), 0))
            for k in range(2 * n)
        ],
        [pl.BlockSpec((1, 2 * half), lambda i, m: (0, 0))],
        [((1, 2 * half), F32)],
        (scal, x, *parts),
        "gain_back",
    )[0]


def seq_sums(sums):
    peers = lax.axis_size("seq")
    at = lax.axis_index("seq")
    for bit in bits_of(peers)[::-1]:
        half = sums.shape[1] // 2
        upper = (at & bit) != 0
        low_part, high_part = sums[:, :half], sums[:, half:]
        kept = jnp.where(upper, high_part, low_part)
        sums = kept + swap(jnp.where(upper, low_part, high_part), bit, "seq")
    return sums


def scattered(grad, dim):
    return lax.psum_scatter(grad, "seq", scatter_dimension=dim, tiled=True)


def on_device(
    block_input, norm_one, w_query, w_key, w_value, w_out, norm_two, w_gate, w_up, w_down,
    starts, cotangent,
):
    tokens, width = block_input.shape
    hid = w_gate.shape[1]
    n = lax.axis_size("tp")
    me = lax.axis_index("tp")
    peers = lax.axis_size("seq")
    at = lax.axis_index("seq")
    rows = tokens // n
    odd = (at & 1) != 0
    scal = jnp.stack([me, at & 1]).astype(jnp.int32)
    gain_one, gain_two = norm_one[None, :], norm_two[None, :]

    order = to_relative(jnp.arange(tokens, dtype=jnp.int32), me, n)
    starts_here = to_relative(starts, me, n)
    positions = (at * tokens + order - starts_here).astype(F32)
    freqs = 10000.0 ** (-2.0 * jnp.arange(HEAD // 2, dtype=F32) / HEAD)
    angles = positions[:, None] * freqs[None, :]
    cosine, sine = jnp.cos(angles), jnp.sin(angles)
    cosine, sine = jnp.concatenate([cosine, cosine], 1), jnp.concatenate([-sine, sine], 1)
    low = jnp.maximum(starts_here - (at - 2) * tokens, order + 2 * tokens - WINDOW + 1)[None, :]

    low_wide = jnp.broadcast_to(low.reshape(tokens, 1), (tokens, HEAD))
    hidden_one, packed_all, *packed = project_keys(scal, block_input, gain_one, w_key, w_value, cosine, sine, n)

    right_two = [(i, i + 2) for i in range(peers - 2)]
    left_two = [(i + 2, i) for i in range(peers - 2)]
    to_odd = [(i, i + 1) for i in range(0, peers, 2)]
    to_even = [(i + 1, i) for i in range(0, peers, 2)]
    query = project_query(scal, hidden_one, w_query, cosine, sine, n)

    segments, attended, lse = [], [], []
    twos = [lax.ppermute(own, "seq", right_two) for own in packed]
    across_all = lax.ppermute(packed_all, "seq", to_odd)
    for g, own in enumerate(packed):
        two = tied(twos[g], attended[g - 1] if g else query)
        segments.append((two, across_all, lax.ppermute(two, "seq", to_even), own))
        if g < GROUPS - 1:
            out, peak = attend(scal, g, query, segments[g], low_wide, n, 0, n)
            attended.append(out)
            lse.append(peak)
    some = attend(scal, g, query, segments[g], low_wide, n, n - 1, 1)
    last_part = project_sum(scal, attended + [some[0]], w_out, n, "project_out", n - 1, 1)
    out, peak = attend(scal, g, query, segments[g], low_wide, n, 0, n - 1, into=tied(some, last_part))
    attended.append(out)
    lse.append(peak)
    parts = project_sum(scal, attended, w_out, n, "project_out", 0, n - 1)
    sent, kept = sum_first(list(parts) + list(last_part), n)
    sent, cot_later = lax.optimization_barrier((sent, cotangent))
    terms = sum_second(sent, kept, n)
    cot, d_act = project_cotangent(scal, cot_later, w_down, n)
    own_f32, own_half = ((rows, width), F32), ((rows, width // 2), BF16)
    mid, *hidden_own = own_rows(
        mid_kernel, scal, [own_f32, own_half, own_half], (block_input, gain_two), tied(terms, (cot, d_act)), "mid"
    )
    hidden_halves = all_blocks(hidden_own, n)
    weights = (w_gate.T, w_up.T)
    whole, own_part = mlp(scal, hidden_halves, d_act, *weights, n, 0, 1)
    whole, last_part = mlp(scal, hidden_halves, d_act, *weights, n, n - 1, 1, into=whole)
    whole, parts = mlp(scal, hidden_halves, d_act, *weights, n, 1, n - 2, into=tied(whole, last_part))
    hidden_two, activation, d_gate, d_up = whole
    parts = list(own_part) + list(parts) + list(last_part)

    d_two_sent, d_two_kept = sum_first(parts, n)
    d_two_sent, activation = lax.optimization_barrier((d_two_sent, activation))
    grad_down = outer(scal, [activation], cot, "grad_down")
    grad_down = scattered(grad_down, 1)
    d_hidden_two = sum_second(d_two_sent, d_two_kept, n)
    out_parts = project_sum(scal, [activation], w_down, n, "project_down")
    d_hidden_two = tied(d_hidden_two, out_parts)
    gain_row = ((1, width), F32)
    d_mid, *d_mid_own, d_gain_two = own_rows(
        d_mid_kernel, scal, [own_f32, own_half, own_half, gain_row], (mid, gain_two, cotangent), d_hidden_two, "d_mid"
    )
    d_mid_halves = all_blocks(d_mid_own, n)
    d_gate, d_up = tied((d_gate, d_up), (d_mid_halves[0][2], d_mid_halves[1][1]))
    grad_gate = outer(scal, [d_gate], hidden_two, "grad_gate")
    grad_up = outer(scal, [d_up], hidden_two, "grad_up")
    d_mid_halves = tied(d_mid_halves, (grad_gate, grad_up))
    grad_gate = scattered(grad_gate, 1)
    out_parts = tied(out_parts, d_mid_halves)
    out_sent, out_kept = sum_first(out_parts, n)
    d_mid_low, d_attended = project_back(scal, d_mid_halves, w_out, n)

    def sent_back(d_two, d_one):
        across = swap(d_one, 1, "seq")
        sent = (d_two.astype(F32) + jnp.where(odd, across.astype(F32), 0.0)).astype(BF16)
        return across, sent

    def back(g, d_attended):
        return attend_back(scal, g, query, segments[g], low, attended[g], d_attended, lse[g], cosine, sine, n)

    d_attended, out_sent = lax.optimization_barrier((d_attended, out_sent))
    out_terms = sum_second(out_sent, out_kept, n)
    grad_out = scattered(outer(scal, attended, d_mid_low, "grad_out"), 1)
    dq, d_two, d_one, d_own = back(0, d_attended)
    across, sent = sent_back(d_two, d_one)
    d_attended, sent, across = lax.optimization_barrier((d_attended, sent, across))
    back_two = lax.ppermute(sent, "seq", left_two)
    dq_1, d_two_1, d_one_1, d_own_1 = back(1, d_attended)
    d_one_1, back_two, out_terms = lax.optimization_barrier((d_one_1, back_two, out_terms))
    out_own = own_rows(output_kernel, scal, [own_half, own_half], (mid,), out_terms, "output")
    out_halves = all_blocks(out_own, n)
    across_1, sent_1 = sent_back(d_two_1, d_one_1)
    sent_1, across_1, back_two = lax.optimization_barrier((sent_1, across_1, back_two))
    back_two_1 = lax.ppermute(sent_1, "seq", left_two)
    back_two = tied(back_two, (out_halves[0][2], out_halves[1][1]))
    first = finish(scal, d_own, across, back_two, dq, cosine, sine, n)
    output = place(scal, out_halves, tuple(range(n)), BF16, n)
    back_two_1 = tied(back_two_1, output)
    grad_up = scattered(tied(grad_up, back_two_1), 1)
    second = finish(scal, d_own_1, across_1, back_two_1, dq_1, cosine, sine, n)
    weights = (w_query, w_key, w_value)
    last_part = project_one_back(scal, [first, second], weights, n, n - 1, 1)
    parts = project_one_back(scal, tied([first, second], last_part), weights, n, 0, n - 1)
    parts = list(parts) + list(last_part)
    d_one_sent, d_one_kept = sum_first(parts, n)
    grad_first = outer(scal, [hidden_one], tied(first, last_part), "grad_first")
    d_one_sent, parts, grad_first = lax.optimization_barrier((d_one_sent, parts, grad_first))
    d_hidden_one = sum_second(d_one_sent, d_one_kept, n)
    d_gain_one = gain_back(scal, block_input, parts, n)
    d_hidden_one = tied(d_hidden_one, d_gain_one)
    input_grad, *input_own_halves = own_rows(
        input_kernel, scal, [own_f32, own_half, own_half], (block_input, gain_one, d_mid), d_hidden_one, "input"
    )
    input_halves = all_blocks(input_own_halves, n)
    near = (input_halves[0][2], input_halves[1][1])
    second, gains = tied((second, jnp.concatenate([d_gain_one, d_gain_two], axis=0)), near)
    grad_second = outer(scal, [hidden_one], second, "grad_second")
    gains = seq_sums(gains)
    for bit in bits_of(n):
        gains = gains + swap(gains, bit)
    early, late = tuple(range(n - 1)), (n - 1,)
    early_halves = tied([side[: n - 1] for side in input_halves], (grad_first, grad_second))
    placed = place(scal, early_halves, early, F32, n, own=input_grad)
    grad_input = place(scal, input_halves, late, F32, n, whole=placed)
    grad_first, grad_second = scattered(grad_first, 0), scattered(grad_second, 0)

    grads, after = [], input_own_halves
    for grad in (grad_down, grad_gate, grad_out):
        after = tied(grad, after)
        grads.append(after)
    after = (after, placed)
    for grad in (grad_up, grad_first):
        after = tied(grad, after)
        grads.append(after)
    grad_second = tied(grad_second, (after, grad_input))
    grad_down, grad_gate, grad_out, grad_up, grad_first = grads
    part = w_query.shape[1] // GROUPS
    grad_query, grad_key, grad_value = (
        jnp.concatenate([g[:, k * part : (k + 1) * part] for g in (grad_first, grad_second)], axis=1).astype(F32)
        for k in range(3)
    )
    return (
        output, grad_input, gains[0], grad_query, grad_key, grad_value, grad_out.astype(F32), gains[1],
        grad_gate.T.astype(F32), grad_up.T.astype(F32), grad_down.astype(F32),
    )


def solution(mesh):
    in_specs = (
        P("seq", None), P(), P(None, "tp"), P(None, "tp"), P(None, "tp"), P("tp", None), P(),
        P(None, "tp"), P(None, "tp"), P("tp", None), P("seq"), P("seq", None),
    )
    out_specs = (
        P("seq", None), P("seq", None), P("seq"), P("seq", "tp"), P("seq", "tp"), P("seq", "tp"),
        P("tp", "seq"), P("seq"), P("seq", "tp"), P("seq", "tp"), P("tp", "seq"),
    )
    return jax.shard_map(
        on_device, mesh=mesh, in_specs=in_specs, out_specs=out_specs, check_vma=False
    )
```

```python
import jax
import jax.numpy as jnp
from jax import lax
from jax.experimental import pallas as pl
from jax.experimental.pallas import tpu as pltpu
from jax.sharding import PartitionSpec as P

HEAD = 128
WINDOW = 2048
LOG2E = 1.4426950408889634
SCALE = HEAD ** (-0.5)
NEG = -1e30
F32 = jnp.float32
BF16 = jnp.bfloat16
MIB = 1024 * 1024
STEPS = 2
GROUPS = 2

NN = (((1,), (0,)), ((), ()))
NT = (((1,), (1,)), ((), ()))
TN = (((0,), (0,)), ((), ()))


def mm(a, b, dims=NN):
    return lax.dot_general(a, b, dims, preferred_element_type=F32)


def tied(values, after):
    return lax.optimization_barrier((values, after))[0]


def call(body, grid, in_specs, out_specs, outs, args, name, scratch=(), vmem=48, into=(), weight=0):
    count = len(args)
    if into:
        inner = body
        body = lambda *refs: inner(*refs[:count], *refs[count + len(into) :])
    return pl.pallas_call(
        body,
        grid_spec=pltpu.PrefetchScalarGridSpec(
            num_scalar_prefetch=1,
            grid=grid,
            in_specs=list(in_specs) + [pl.BlockSpec(memory_space=pl.ANY)] * len(into),
            out_specs=out_specs,
            scratch_shapes=list(scratch),
        ),
        input_output_aliases={count + k: k for k in range(len(into))},
        out_shape=[jax.ShapeDtypeStruct(shape, kind) for shape, kind in outs],
        compiler_params=pltpu.CompilerParams(vmem_limit_bytes=vmem * MIB),
        cost_estimate=pl.CostEstimate(flops=weight, bytes_accessed=0, transcendentals=0),
        name=name,
    )(*args, *into)


RESIDENT = pl.BlockSpec(memory_space=pltpu.VMEM)


def fixed(shape):
    return pl.BlockSpec(shape, lambda *_: (0,) * len(shape), pipeline_mode=pl.Buffered(1))


def to_relative(array, me, n):
    rows = array.shape[0] // n
    return jnp.concatenate(
        [lax.dynamic_slice_in_dim(array, (r ^ me) * rows, rows, 0) for r in range(n)], axis=0
    )


def swap(array, bit, axis="tp"):
    size = lax.axis_size(axis)
    return lax.ppermute(array, axis, [(i, i ^ bit) for i in range(size)])


def bits_of(n):
    return [1 << b for b in range(n.bit_length() - 1)]


def sum_first(parts, n):
    cut = lambda r, side: parts[2 * r + side]
    if n == 4:
        three_left, three_right = swap(cut(3, 0), 1), swap(cut(3, 1), 2)
        one_left, two_right = swap(cut(1, 0), 1), swap(cut(2, 1), 2)
        one_right = (cut(1, 1).astype(F32) + three_right.astype(F32)).astype(BF16)
        two_left = (cut(2, 0).astype(F32) + three_left.astype(F32)).astype(BF16)
        return (one_right, two_left), ([cut(0, 0), one_left], [cut(0, 1), two_right])
    sides = []
    rows = parts[0].shape[0]
    for side, order in enumerate((bits_of(n), bits_of(n)[::-1])):
        held = {r: cut(r, side) for r in range(n)}
        for bit in order:
            sent = [r for r in held if r & bit]
            got = swap(jnp.concatenate([held[r] for r in sent]).astype(BF16), bit)
            held = {
                r ^ bit: held[r ^ bit].astype(F32) + got[k * rows : (k + 1) * rows].astype(F32)
                for k, r in enumerate(sent)
            }
        sides.append(held[0])
    return tuple(sides), ([], [])


def sum_second(sent, kept, n):
    if n == 4:
        one_right, two_left = swap(sent[0], 1), swap(sent[1], 2)
        return kept[0] + [two_left], kept[1] + [one_right]
    return [sent[0]], [sent[1]]


def all_blocks(own, n):
    left, right = own
    if n == 4:
        one_right, two_left = swap(right, 1), swap(left, 2)
        one_left, two_right = swap(left, 1), swap(right, 2)
        three_left, three_right = swap(two_left, 1), swap(one_right, 2)
        return [left, one_left, two_left, three_left], [right, one_right, two_right, three_right]
    sides = []
    rows = left.shape[0]
    for side, order in enumerate((bits_of(n)[::-1], bits_of(n))):
        held = {0: own[side]}
        for bit in order:
            have = sorted(held)
            got = swap(jnp.concatenate([held[r] for r in have]), bit)
            for k, r in enumerate(have):
                held[r ^ bit] = got[k * rows : (k + 1) * rows]
        sides.append([held[r] for r in range(n)])
    return sides[0], sides[1]


def rotated(a, cosine, sine):
    return a * cosine + pltpu.roll(a, HEAD // 2, 1) * sine


def total(refs):
    out = refs[0][...].astype(F32)
    for ref in refs[1:]:
        out = out + ref[...].astype(F32)
    return out


def heads_of(width):
    return [slice(h * HEAD, (h + 1) * HEAD) for h in range(width // HEAD)]


def keys_kernel(me_ref, x_ref, gain_ref, wk_ref, wv_ref, cos_ref, sin_ref, h_ref, all_ref, *kv_refs):
    x = x_ref[...].astype(F32)
    factor = lax.rsqrt(jnp.mean(x * x, axis=-1, keepdims=True) + 1e-06)
    hidden = (x * factor * gain_ref[...]).astype(BF16)
    h_ref[...] = hidden
    cosine, sine = cos_ref[...], sin_ref[...]
    for g, kv_ref in enumerate(kv_refs):
        width = kv_ref.shape[2]
        cols = slice(g * width, (g + 1) * width)
        key = mm(hidden, wk_ref[:, cols])
        for cut in heads_of(width):
            kv_ref[0, :, cut] = rotated(key[:, cut], cosine, sine).astype(BF16)
        kv_ref[1] = mm(hidden, wv_ref[:, cols]).astype(BF16)
        all_ref[2 * g : 2 * g + 2] = kv_ref[...]


def project_keys(scal, x, gain, wk, wv, cosine, sine, n):
    tokens, width = x.shape
    local = wk.shape[1]
    rows, part = tokens // n, local // GROUPS
    mine = lambda r, m: (r, 0)
    return call(
        keys_kernel,
        (n,),
        [
            pl.BlockSpec((rows, width), lambda r, m: (r ^ m[0], 0)),
            fixed((1, width)),
            fixed((width, local)),
            fixed((width, local)),
            pl.BlockSpec((rows, HEAD), mine),
            pl.BlockSpec((rows, HEAD), mine),
        ],
        [pl.BlockSpec((rows, width), mine)]
        + [pl.BlockSpec((2 * GROUPS, rows, part), lambda r, m: (0, r, 0))]
        + [pl.BlockSpec((2, rows, part), lambda r, m: (0, r, 0))] * GROUPS,
        [((tokens, width), BF16), ((2 * GROUPS, tokens, part), BF16)] + [((2, tokens, part), BF16)] * GROUPS,
        (scal, x, gain, wk, wv, cosine, sine),
        "project_keys",
    )


def query_kernel(me_ref, h_ref, w_ref, cos_ref, sin_ref, q_ref):
    pre = mm(h_ref[...], w_ref[...])
    for cut in heads_of(pre.shape[1]):
        q_ref[:, cut] = rotated(pre[:, cut], cos_ref[...], sin_ref[...]).astype(BF16)


def project_query(scal, hidden, wq, cosine, sine, n):
    tokens, width = hidden.shape
    local = wq.shape[1]
    rows = tokens // n
    mine = lambda r, m: (r, 0)
    return call(
        query_kernel,
        (n,),
        [
            pl.BlockSpec((rows, width), mine),
            fixed((width, local)),
            pl.BlockSpec((rows, HEAD), mine),
            pl.BlockSpec((rows, HEAD), mine),
        ],
        [pl.BlockSpec((rows, local), mine)],
        [((tokens, local), BF16)],
        (scal, hidden, wq, cosine, sine),
        "project_query",
    )[0]


def act_kernel(me_ref, cot_ref, w_ref, rel_ref, d_ref):
    cot = cot_ref[...]
    rel_ref[...] = cot
    d_ref[...] = mm(cot, w_ref[...], NT)


def project_cotangent(scal, cot, w_down, n):
    tokens, width = cot.shape
    hid = w_down.shape[0]
    rows = tokens // n
    mine = lambda r, m: (r, 0)
    return call(
        act_kernel,
        (n,),
        [pl.BlockSpec((rows, width), lambda r, m: (r ^ m[0], 0)), fixed((hid, width))],
        [pl.BlockSpec((rows, width), mine), pl.BlockSpec((rows, hid), mine)],
        [((tokens, width), BF16), ((tokens, hid), F32)],
        (scal, cot, w_down),
        "project_cotangent",
    )


def masked(s, first, low, query_at, diagonal):
    key_at = first + lax.broadcasted_iota(jnp.int32, s.shape, 0)
    keep = key_at >= low
    if diagonal:
        keep = keep & (key_at <= query_at)
    return jnp.where(keep, s, NEG)


def lay_window(n, rows, me, odd, which, two_ref, odd_ref, even_ref, own_ref, put):
    for seg, refs in enumerate(((two_ref,), (odd_ref, even_ref), (own_ref,))):
        for sub in range(n):
            here = pl.ds(pl.multiple_of((sub ^ me) * rows, rows), rows)
            at = slice((seg * n + sub) * rows, (seg * n + sub + 1) * rows)
            if len(refs) == 1:
                put(at, refs[0][which, here, :])
            else:
                put(at, jnp.where(odd != 0, refs[0][which, here, :], refs[1][which, here, :]))


def lanes(array):
    return [array[:, j * HEAD : (j + 1) * HEAD] for j in range(array.shape[1] // HEAD)]


def attend_kernel(n, at, s_ref_, q_ref, two_ref, odd_ref, even_ref, own_ref, low_ref, o_ref, lse_ref, s_ref, k_ref, v_ref):
    rows = q_ref.shape[0]
    me, odd = s_ref_[0], s_ref_[1]
    start = ((pl.program_id(1) + at) ^ me) * rows
    chunks = 2 * n + 1

    @pl.when(pl.program_id(1) == 0)
    def _():
        def put_key(at, block):
            k_ref[at, :] = block

        def put_value(at, block):
            v_ref[at, :] = block

        window = (two_ref, odd_ref, even_ref, own_ref)
        lay_window(n, rows, me, odd, 0, *window, put_key)
        lay_window(n, rows, me, odd, 1, *window, put_value)

    q = q_ref[...]
    low = low_ref[...] - start
    low = jnp.concatenate([low] * (rows // HEAD), axis=1)
    key_at = lax.broadcasted_iota(jnp.int32, (rows, rows), 1)
    query_at = lax.broadcasted_iota(jnp.int32, (rows, rows), 0)
    top = jnp.full((rows, HEAD), NEG, F32)
    for c in range(chunks):
        here = pl.ds(pl.multiple_of(start + c * rows, rows), rows)
        s = mm(q, k_ref[here, :], NT)
        keep = key_at >= low - c * rows
        if c == chunks - 1:
            keep = keep & (key_at <= query_at)
        s = jnp.where(keep, s, NEG)
        s_ref[:, c * rows : (c + 1) * rows] = s
        for lane in lanes(s):
            top = jnp.maximum(top, lane)
    top = jnp.max(top, axis=1, keepdims=True) * (SCALE * LOG2E)
    whole = jnp.zeros((rows, HEAD), F32)
    acc = jnp.zeros((rows, HEAD), F32)
    for c in range(chunks):
        here = pl.ds(pl.multiple_of(start + c * rows, rows), rows)
        p = jnp.exp2(s_ref[:, c * rows : (c + 1) * rows] * (SCALE * LOG2E) - top)
        for lane in lanes(p):
            whole = whole + lane
        acc = acc + mm(p.astype(BF16), v_ref[here, :])
    whole = jnp.sum(whole, axis=1, keepdims=True)
    o_ref[...] = (acc / whole).astype(BF16)
    lse = jnp.broadcast_to(top + jnp.log2(whole), (rows, HEAD)).T
    lse_ref[...] = lse[:1, :].reshape(lse_ref.shape)


def attend(scal, g, q, segments, low, n, at, count, into=()):
    tokens = q.shape[0]
    part = segments[0].shape[2]
    heads, rows = part // HEAD, tokens // n
    pairs = heads * tokens * (2 * tokens + rows)
    segment = pl.BlockSpec((2, tokens, HEAD), lambda h, r, m: (0, 0, h))
    across = pl.BlockSpec((2, tokens, HEAD), lambda h, r, m: (g, 0, h))
    return call(
        lambda *refs: attend_kernel(n, at, *refs),
        (heads, count),
        [pl.BlockSpec((rows, HEAD), lambda h, r, m: (r + at, g * heads + h))]
        + [segment, across, segment, segment]
        + [pl.BlockSpec((rows, HEAD), lambda h, r, m: (r + at, 0))],
        [
            pl.BlockSpec((rows, HEAD), lambda h, r, m: (r + at, h)),
            pl.BlockSpec((1, 1, rows), lambda h, r, m: (h, 0, r + at)),
        ],
        [((tokens, part), BF16), ((heads, 1, tokens), F32)],
        (scal, q, *segments, low),
        "attend",
        scratch=[
            pltpu.VMEM((rows, (2 * n + 1) * rows), F32),
            pltpu.VMEM((3 * tokens, HEAD), BF16),
            pltpu.VMEM((3 * tokens, HEAD), BF16),
        ],
        into=into,
    )


def attend_back_kernel(
    n, s_ref_, q_ref, two_ref, odd_ref, even_ref, own_ref, low_ref, o_ref, do_ref, lse_ref, cos_ref, sin_ref,
    dq_ref, d_two_ref, d_one_ref, d_own_ref, dk_acc, dv_acc, k_ref, kt_ref, v_ref,
):
    rows = q_ref.shape[0]
    me, odd = s_ref_[0], s_ref_[1]
    r = pl.program_id(1)
    rb = r ^ me
    chunks = 2 * n + 1

    @pl.when(r == 0)
    def _():
        def put_key(at, block):
            k_ref[at, :] = block
            kt_ref[:, at] = block.T
            dk_acc[at, :] = jnp.zeros((rows, HEAD), F32)
            dv_acc[at, :] = jnp.zeros((rows, HEAD), F32)

        def put_value(at, block):
            v_ref[at, :] = block

        window = (two_ref, odd_ref, even_ref, own_ref)
        lay_window(n, rows, me, odd, 0, *window, put_key)
        lay_window(n, rows, me, odd, 1, *window, put_value)

    q, do = q_ref[...], do_ref[...]
    low = low_ref[...]
    lse = lse_ref[...].reshape(1, rows)
    delta = jnp.sum((do.astype(F32) * o_ref[...].astype(F32)).T, axis=0, keepdims=True)
    query_at = (rb + 2 * n) * rows + lax.broadcasted_iota(jnp.int32, (1, rows), 1)
    steps = []
    for c in range(chunks):
        first = pl.multiple_of((rb + c) * rows, rows)
        here = pl.ds(first, rows)
        s = mm(k_ref[here, :], q, NT) * (SCALE * LOG2E)
        s = masked(s, first, low, query_at, c == chunks - 1)
        p = jnp.exp2(s - lse)
        dp = mm(v_ref[here, :], do, NT)
        steps.append((here, p.astype(BF16), (p * (dp - delta)).astype(BF16)))
    dqt = jnp.zeros((HEAD, rows), F32)
    for here, p, ds in steps:
        dv_acc[here, :] += mm(p, do)
        dk_acc[here, :] += mm(ds, q)
        dqt = dqt + mm(kt_ref[:, here], ds)
    dq_ref[...] = rotated(dqt.T * SCALE, cos_ref[...], -sin_ref[...]).astype(BF16)

    @pl.when(r == n - 1)
    def _():
        for seg, out_ref in enumerate((d_two_ref, d_one_ref, d_own_ref)):
            for sub in range(n):
                here = pl.ds(pl.multiple_of((sub ^ me) * rows, rows), rows)
                at = slice((seg * n + sub) * rows, (seg * n + sub + 1) * rows)
                out_ref[0, here, :] = (dk_acc[at, :] * SCALE).astype(BF16)
                out_ref[1, here, :] = dv_acc[at, :].astype(BF16)


def attend_back(scal, g, q, segments, low, attended, d_attended, lse, cosine, sine, n):
    tokens = q.shape[0]
    part = segments[0].shape[2]
    heads, rows = part // HEAD, tokens // n
    pairs = heads * tokens * (2 * tokens + rows)
    block = pl.BlockSpec((rows, HEAD), lambda h, r, m: (r, h))
    shared = pl.BlockSpec((rows, HEAD), lambda h, r, m: (r, g * heads + h))
    segment = pl.BlockSpec((2, tokens, HEAD), lambda h, r, m: (0, 0, h))
    across = pl.BlockSpec((2, tokens, HEAD), lambda h, r, m: (g, 0, h))
    table = pl.BlockSpec((rows, HEAD), lambda h, r, m: (r, 0))
    return call(
        lambda *refs: attend_back_kernel(n, *refs),
        (heads, n),
        [shared]
        + [segment, across, segment, segment]
        + [
            pl.BlockSpec((1, rows), lambda h, r, m: (0, r)),
            block,
            shared,
            pl.BlockSpec((1, 1, rows), lambda h, r, m: (h, 0, r)),
            table,
            table,
        ],
        [block] + [segment] * 3,
        [((tokens, part), BF16)] + [((2, tokens, part), BF16)] * 3,
        (scal, q, *segments, low, attended, d_attended, lse, cosine, sine),
        "attend_back",
        weight=69_000_000_000,
        scratch=[
            pltpu.VMEM((3 * tokens, HEAD), F32),
            pltpu.VMEM((3 * tokens, HEAD), F32),
            pltpu.VMEM((3 * tokens, HEAD), BF16),
            pltpu.VMEM((HEAD, 3 * tokens), BF16),
            pltpu.VMEM((3 * tokens, HEAD), BF16),
        ],
    )


def put_part(value, refs):
    half = refs[0].shape[1]
    value = value.astype(BF16)
    for r in range(len(refs) // 2):

        @pl.when(pl.program_id(0) == r)
        def _():
            refs[2 * r][...] = value[:, :half]
            refs[2 * r + 1][...] = value[:, half:]


def part_outs(n, rows, width):
    half = (rows, width // 2)
    return [pl.BlockSpec(half, lambda *_: (0, 0))] * (2 * n), [(half, BF16)] * (2 * n)


def sum_kernel(count, me_ref, *refs):
    arrays, w_ref, part_refs = refs[:count], refs[count], refs[count + 1 :]
    deep = arrays[0].shape[1]
    acc = mm(arrays[0][...], w_ref[:deep, :])
    for g in range(1, count):
        acc = acc + mm(arrays[g][...], w_ref[g * deep : (g + 1) * deep, :])
    put_part(acc, part_refs)


def project_sum(scal, arrays, weight, n, name, at=0, count=None):
    tokens, deep = arrays[0].shape
    width = weight.shape[1]
    rows = tokens // n
    count = n if count is None else count
    specs, outs = part_outs(count, rows, width)
    return call(
        lambda *refs: sum_kernel(len(arrays), *refs),
        (count,),
        [pl.BlockSpec((rows, deep), lambda r, m: (r + at, 0))] * len(arrays) + [fixed(weight.shape)],
        specs,
        outs,
        (scal, *arrays, weight),
        name,
    )


def own_rows(kernel, scal, outs, args, lists, name):
    rows, half = lists[0][0].shape
    flat = tuple(lists[0]) + tuple(lists[1])
    count = len(args)

    def body(_, *refs):
        left = refs[count : count + len(lists[0])]
        right = refs[count + len(lists[0]) : count + len(flat)]
        summed = jnp.concatenate([total(left), total(right)], axis=1)
        kernel(summed, *refs[:count], *refs[count + len(flat) :])

    def spec(shape):
        if shape[0] == 1:
            return pl.BlockSpec(shape, lambda i, m: (0, 0))
        if shape[0] == rows:
            return pl.BlockSpec((rows // STEPS, shape[1]), lambda i, m: (i, 0))
        return pl.BlockSpec((rows // STEPS, shape[1]), lambda i, m: (m[0] * STEPS + i, 0))

    return call(
        body,
        (STEPS,),
        [spec(a.shape) for a in args] + [spec((rows, half))] * len(flat),
        [spec(shape) for shape, _ in outs],
        outs,
        (scal, *args, *flat),
        name,
    )


def mid_kernel(summed, x_ref, gain_ref, mid_ref, left_ref, right_ref):
    half = left_ref.shape[1]
    mid = x_ref[...].astype(F32) + summed
    mid_ref[...] = mid
    factor = lax.rsqrt(jnp.mean(mid * mid, axis=-1, keepdims=True) + 1e-06)
    hidden = (mid * factor * gain_ref[...]).astype(BF16)
    left_ref[...] = hidden[:, :half]
    right_ref[...] = hidden[:, half:]


def add_rows(out_ref, values):
    @pl.when(pl.program_id(0) == 0)
    def _():
        out_ref[...] = jnp.zeros_like(out_ref)

    out_ref[...] += jnp.sum(values, axis=0, keepdims=True)


def back_norm(d_hidden, values, gain, d_gain_ref=None):
    factor = lax.rsqrt(jnp.mean(values * values, axis=-1, keepdims=True) + 1e-06)
    normed = values * factor
    if d_gain_ref is not None:
        add_rows(d_gain_ref, d_hidden * normed)
    e = d_hidden * gain
    return factor * (e - normed * jnp.mean(e * normed, axis=-1, keepdims=True))


def d_mid_kernel(d_hidden, mid_ref, gain_ref, cot_ref, d_mid_ref, left_ref, right_ref, d_gain_ref):
    half = left_ref.shape[1]
    d_mid = cot_ref[...].astype(F32) + back_norm(d_hidden, mid_ref[...], gain_ref[...], d_gain_ref)
    d_mid_ref[...] = d_mid
    left_ref[...] = d_mid[:, :half].astype(BF16)
    right_ref[...] = d_mid[:, half:].astype(BF16)


def input_kernel(d_hidden, x_ref, gain_ref, d_mid_ref, own_ref, left_ref, right_ref):
    half = left_ref.shape[1]
    grad = d_mid_ref[...] + back_norm(d_hidden, x_ref[...].astype(F32), gain_ref[...])
    own_ref[...] = grad
    left_ref[...] = grad[:, :half].astype(BF16)
    right_ref[...] = grad[:, half:].astype(BF16)


def output_kernel(summed, mid_ref, left_ref, right_ref):
    half = left_ref.shape[1]
    out = (mid_ref[...] + summed).astype(BF16)
    left_ref[...] = out[:, :half]
    right_ref[...] = out[:, half:]


def lay_block(n, left_refs, right_refs, whole_ref):
    half = left_refs[0].shape[1]
    for r in range(n):

        @pl.when(pl.program_id(0) == r)
        def _():
            whole_ref[:, :half] = left_refs[r][...].astype(whole_ref.dtype)
            whole_ref[:, half:] = right_refs[r][...].astype(whole_ref.dtype)


def mlp_kernel(n, me_ref, *refs):
    left, right = refs[:n], refs[n : 2 * n]
    d_act_ref, wg_ref, wu_ref, h_ref, act_ref, dg_ref, du_ref = refs[2 * n : 2 * n + 7]
    lay_block(n, left, right, h_ref)
    hidden = h_ref[...]
    gate = mm(hidden, wg_ref[...], NT)
    up = mm(hidden, wu_ref[...], NT)
    d_act = d_act_ref[...]
    s = 1.0 / (1.0 + jnp.exp(-gate))
    silu = gate * s
    act_ref[...] = (silu * up).astype(BF16)
    d_gate = (d_act * up * s * (1.0 + gate * (1.0 - s))).astype(BF16)
    d_up = (d_act * silu).astype(BF16)
    dg_ref[...] = d_gate
    du_ref[...] = d_up
    put_part(mm(d_gate, wg_ref[...]) + mm(d_up, wu_ref[...]), refs[2 * n + 7 :])


def mlp(scal, halves, d_act, w_gate, w_up, n, at, count, into=()):
    left, right = (side[at : at + count] for side in halves)
    rows, half = left[0].shape
    hid, width = w_gate.shape
    tokens = rows * n
    mine = lambda r, m: (r + at, 0)
    specs, outs = part_outs(count, rows, width)
    results = call(
        lambda *refs: mlp_kernel(count, *refs),
        (count,),
        [fixed((rows, half))] * (2 * count)
        + [pl.BlockSpec((rows, hid), mine), RESIDENT, RESIDENT],
        [pl.BlockSpec((rows, width), mine)] + [pl.BlockSpec((rows, hid), mine)] * 3 + specs,
        [((tokens, width), BF16)] + [((tokens, hid), BF16)] * 3 + outs,
        (scal, *left, *right, d_act, w_gate, w_up),
        "mlp",
        vmem=50,
        into=into,
    )
    return results[:4], results[4:]


def outer_kernel(me_ref, *refs):
    *left, right_ref, out_ref = refs
    deep = left[0].shape[1]
    for g, ref in enumerate(left):
        out_ref[g * deep : (g + 1) * deep, :] = mm(ref[...], right_ref[...], TN).astype(BF16)


def outer(scal, left, right, name):
    tokens, deep = left[0].shape
    width = right.shape[1]
    steps = 4 if width % 512 == 0 else 3
    step = width // steps
    return call(
        outer_kernel,
        (steps,),
        [fixed((tokens, deep))] * len(left) + [pl.BlockSpec((tokens, step), lambda j, m: (0, j))],
        [pl.BlockSpec((len(left) * deep, step), lambda j, m: (0, j))],
        [((len(left) * deep, width), BF16)],
        (scal, *left, right),
        name,
    )[0]


def d_attended_kernel(n, me_ref, *refs):
    left, right = refs[:n], refs[n : 2 * n]
    w_ref, low_ref, d_ref = refs[2 * n :]
    lay_block(n, left, right, low_ref)
    d_ref[...] = mm(low_ref[...], w_ref[...], NT).astype(BF16)


def project_back(scal, halves, w_out, n):
    rows, half = halves[0][0].shape
    local, width = w_out.shape
    tokens = rows * n
    mine = lambda r, m: (r, 0)
    return call(
        lambda *refs: d_attended_kernel(n, *refs),
        (n,),
        [fixed((rows, half))] * (2 * n) + [fixed((local, width))],
        [pl.BlockSpec((rows, width), mine), pl.BlockSpec((rows, local), mine)],
        [((tokens, width), BF16), ((tokens, local), BF16)],
        (scal, *halves[0], *halves[1], w_out),
        "project_back",
    )


def place_kernel(blocks, has_own, me_ref, *refs):
    count = len(blocks)
    left, right, out_ref = refs[:count], refs[count : 2 * count], refs[-1]
    lay_block(count, left, right, out_ref)
    if has_own:

        @pl.when(pl.program_id(0) == 0)
        def _():
            out_ref[...] = refs[2 * count][...]


def place(scal, halves, blocks, kind, n, own=None, whole=None):
    rows, half = halves[0][0].shape
    first = blocks[0]
    arrays = [side[r] for side in halves for r in blocks]
    extra = [] if own is None else [own]
    held = [] if whole is None else [whole]
    return pl.pallas_call(
        lambda *refs: place_kernel(blocks, own is not None, *refs),
        grid_spec=pltpu.PrefetchScalarGridSpec(
            num_scalar_prefetch=1,
            grid=(len(blocks),),
            in_specs=[fixed((rows, half))] * len(arrays)
            + [fixed(e.shape) for e in extra]
            + [pl.BlockSpec(memory_space=pl.ANY)] * len(held),
            out_specs=pl.BlockSpec((rows, 2 * half), lambda r, m: ((r + first) ^ m[0], 0)),
        ),
        out_shape=jax.ShapeDtypeStruct((rows * n, 2 * half), kind),
        input_output_aliases={1 + len(arrays) + len(extra): 0} if held else {},
        compiler_params=pltpu.CompilerParams(vmem_limit_bytes=40 * MIB),
        cost_estimate=pl.CostEstimate(flops=0, bytes_accessed=0, transcendentals=0),
        name="place",
    )(scal, *arrays, *extra, *held)


def finish_kernel(s_ref_, own_ref, across_ref, back_ref, dq_ref, cos_ref, sin_ref, all_ref):
    part = dq_ref.shape[1]
    share = jnp.where(s_ref_[1] != 0, 0.0, 1.0)
    whole = own_ref[...].astype(F32) + back_ref[...].astype(F32) + across_ref[...].astype(F32) * share
    all_ref[:, :part] = dq_ref[...]
    for h, cut in enumerate(heads_of(part)):
        to = slice(part + h * HEAD, part + (h + 1) * HEAD)
        all_ref[:, to] = rotated(whole[0, :, cut], cos_ref[...], -sin_ref[...]).astype(BF16)
    all_ref[:, 2 * part :] = whole[1].astype(BF16)


def finish(scal, own, across, back, dq, cosine, sine, n):
    tokens, part = dq.shape
    rows = tokens // n
    segment = pl.BlockSpec((2, rows, part), lambda r, m: (0, r, 0))
    mine = lambda r, m: (r, 0)
    return call(
        finish_kernel,
        (n,),
        [segment] * 3
        + [pl.BlockSpec((rows, part), mine), pl.BlockSpec((rows, HEAD), mine), pl.BlockSpec((rows, HEAD), mine)],
        [pl.BlockSpec((rows, 3 * part), mine)],
        [((tokens, 3 * part), BF16)],
        (scal, own, across, back, dq, cosine, sine),
        "finish",
    )[0]


def d_one_kernel(me_ref, *refs):
    grads, weights = refs[:GROUPS], refs[GROUPS : GROUPS + 3]
    part = grads[0].shape[1] // 3
    acc = None
    for g, grad in enumerate(grads):
        for k, w_ref in enumerate(weights):
            term = mm(grad[:, k * part : (k + 1) * part], w_ref[:, g * part : (g + 1) * part], NT)
            acc = term if acc is None else acc + term
    put_part(acc, refs[GROUPS + 3 :])


def project_one_back(scal, grads, weights, n, at, count):
    tokens, triple = grads[0].shape
    width, local = weights[0].shape
    rows = tokens // n
    specs, outs = part_outs(count, rows, width)
    return call(
        d_one_kernel,
        (count,),
        [pl.BlockSpec((rows, triple), lambda r, m: (r + at, 0))] * GROUPS + [fixed((width, local))] * 3,
        specs,
        outs,
        (scal, *grads, *weights),
        "project_one_back",
    )


def gain_kernel(n, me_ref, x_ref, *refs):
    parts, gain_ref = refs[:-1], refs[-1]
    half = parts[0].shape[1]
    x = x_ref[...].astype(F32)
    normed = x * lax.rsqrt(jnp.mean(x * x, axis=-1, keepdims=True) + 1e-06)
    part = jnp.concatenate([parts[0][...], parts[1][...]], axis=1)
    for r in range(1, n):
        this = jnp.concatenate([parts[2 * r][...], parts[2 * r + 1][...]], axis=1)
        part = jnp.where(lax.div(pl.program_id(0), STEPS) == r, this, part)
    add_rows(gain_ref, part.astype(F32) * normed)


def gain_back(scal, x, parts, n):
    rows, half = parts[0].shape
    step = rows // STEPS
    return call(
        lambda *refs: gain_kernel(n, *refs),
        (n * STEPS,),
        [pl.BlockSpec((step, 2 * half), lambda i, m: ((lax.div(i, STEPS) ^ m[0]) * STEPS + lax.rem(i, STEPS), 0))]
        + [
            pl.BlockSpec((step, half), lambda i, m, r=k // 2: (jnp.clip(i - r * STEPS, 0, STEPS - 1), 0))
            for k in range(2 * n)
        ],
        [pl.BlockSpec((1, 2 * half), lambda i, m: (0, 0))],
        [((1, 2 * half), F32)],
        (scal, x, *parts),
        "gain_back",
    )[0]


def seq_sums(sums):
    peers = lax.axis_size("seq")
    at = lax.axis_index("seq")
    for bit in bits_of(peers)[::-1]:
        half = sums.shape[1] // 2
        upper = (at & bit) != 0
        low_part, high_part = sums[:, :half], sums[:, half:]
        kept = jnp.where(upper, high_part, low_part)
        sums = kept + swap(jnp.where(upper, low_part, high_part), bit, "seq")
    return sums


def scattered(grad, dim):
    return lax.psum_scatter(grad, "seq", scatter_dimension=dim, tiled=True)


def on_device(
    block_input, norm_one, w_query, w_key, w_value, w_out, norm_two, w_gate, w_up, w_down,
    starts, cotangent,
):
    tokens, width = block_input.shape
    hid = w_gate.shape[1]
    n = lax.axis_size("tp")
    me = lax.axis_index("tp")
    peers = lax.axis_size("seq")
    at = lax.axis_index("seq")
    rows = tokens // n
    odd = (at & 1) != 0
    scal = jnp.stack([me, at & 1]).astype(jnp.int32)
    gain_one, gain_two = norm_one[None, :], norm_two[None, :]

    order = to_relative(jnp.arange(tokens, dtype=jnp.int32), me, n)
    starts_here = to_relative(starts, me, n)
    positions = (at * tokens + order - starts_here).astype(F32)
    freqs = 10000.0 ** (-2.0 * jnp.arange(HEAD // 2, dtype=F32) / HEAD)
    angles = positions[:, None] * freqs[None, :]
    cosine, sine = jnp.cos(angles), jnp.sin(angles)
    cosine, sine = jnp.concatenate([cosine, cosine], 1), jnp.concatenate([-sine, sine], 1)
    low = jnp.maximum(starts_here - (at - 2) * tokens, order + 2 * tokens - WINDOW + 1)[None, :]

    low_wide = jnp.broadcast_to(low.reshape(tokens, 1), (tokens, HEAD))
    hidden_one, packed_all, *packed = project_keys(scal, block_input, gain_one, w_key, w_value, cosine, sine, n)

    right_two = [(i, i + 2) for i in range(peers - 2)]
    left_two = [(i + 2, i) for i in range(peers - 2)]
    to_odd = [(i, i + 1) for i in range(0, peers, 2)]
    to_even = [(i + 1, i) for i in range(0, peers, 2)]
    query = project_query(scal, hidden_one, w_query, cosine, sine, n)

    segments, attended, lse = [], [], []
    twos = [lax.ppermute(own, "seq", right_two) for own in packed]
    across_all = lax.ppermute(packed_all, "seq", to_odd)
    for g, own in enumerate(packed):
        two = tied(twos[g], attended[g - 1] if g else query)
        segments.append((two, across_all, lax.ppermute(two, "seq", to_even), own))
        if g < GROUPS - 1:
            out, peak = attend(scal, g, query, segments[g], low_wide, n, 0, n)
            attended.append(out)
            lse.append(peak)
    some = attend(scal, g, query, segments[g], low_wide, n, n - 1, 1)
    last_part = project_sum(scal, attended + [some[0]], w_out, n, "project_out", n - 1, 1)
    out, peak = attend(scal, g, query, segments[g], low_wide, n, 0, n - 1, into=tied(some, last_part))
    attended.append(out)
    lse.append(peak)
    parts = project_sum(scal, attended, w_out, n, "project_out", 0, n - 1)
    sent, kept = sum_first(list(parts) + list(last_part), n)
    sent, cot_later = lax.optimization_barrier((sent, cotangent))
    terms = sum_second(sent, kept, n)
    cot, d_act = project_cotangent(scal, cot_later, w_down, n)
    own_f32, own_half = ((rows, width), F32), ((rows, width // 2), BF16)
    mid, *hidden_own = own_rows(
        mid_kernel, scal, [own_f32, own_half, own_half], (block_input, gain_two), tied(terms, (cot, d_act)), "mid"
    )
    hidden_halves = all_blocks(hidden_own, n)
    weights = (w_gate.T, w_up.T)
    whole, own_part = mlp(scal, hidden_halves, d_act, *weights, n, 0, 1)
    whole, last_part = mlp(scal, hidden_halves, d_act, *weights, n, n - 1, 1, into=whole)
    whole, parts = mlp(scal, hidden_halves, d_act, *weights, n, 1, n - 2, into=tied(whole, last_part))
    hidden_two, activation, d_gate, d_up = whole
    parts = list(own_part) + list(parts) + list(last_part)

    d_two_sent, d_two_kept = sum_first(parts, n)
    d_two_sent, activation = lax.optimization_barrier((d_two_sent, activation))
    grad_down = outer(scal, [activation], cot, "grad_down")
    grad_down = scattered(grad_down, 1)
    d_hidden_two = sum_second(d_two_sent, d_two_kept, n)
    out_parts = project_sum(scal, [activation], w_down, n, "project_down")
    d_hidden_two = tied(d_hidden_two, out_parts)
    gain_row = ((1, width), F32)
    d_mid, *d_mid_own, d_gain_two = own_rows(
        d_mid_kernel, scal, [own_f32, own_half, own_half, gain_row], (mid, gain_two, cotangent), d_hidden_two, "d_mid"
    )
    d_mid_halves = all_blocks(d_mid_own, n)
    d_gate, d_up = tied((d_gate, d_up), (d_mid_halves[0][2], d_mid_halves[1][1]))
    grad_gate = outer(scal, [d_gate], hidden_two, "grad_gate")
    grad_up = outer(scal, [d_up], hidden_two, "grad_up")
    d_mid_halves = tied(d_mid_halves, (grad_gate, grad_up))
    grad_gate = scattered(grad_gate, 1)
    out_parts = tied(out_parts, d_mid_halves)
    out_sent, out_kept = sum_first(out_parts, n)
    d_mid_low, d_attended = project_back(scal, d_mid_halves, w_out, n)

    def sent_back(d_two, d_one):
        across = swap(d_one, 1, "seq")
        sent = (d_two.astype(F32) + jnp.where(odd, across.astype(F32), 0.0)).astype(BF16)
        return across, sent

    def back(g, d_attended):
        return attend_back(scal, g, query, segments[g], low, attended[g], d_attended, lse[g], cosine, sine, n)

    d_attended, out_sent = lax.optimization_barrier((d_attended, out_sent))
    out_terms = sum_second(out_sent, out_kept, n)
    grad_out = scattered(outer(scal, attended, d_mid_low, "grad_out"), 1)
    dq, d_two, d_one, d_own = back(0, d_attended)
    across, sent = sent_back(d_two, d_one)
    d_attended, sent, across = lax.optimization_barrier((d_attended, sent, across))
    back_two = lax.ppermute(sent, "seq", left_two)
    dq_1, d_two_1, d_one_1, d_own_1 = back(1, d_attended)
    d_one_1, back_two, out_terms = lax.optimization_barrier((d_one_1, back_two, out_terms))
    out_own = own_rows(output_kernel, scal, [own_half, own_half], (mid,), out_terms, "output")
    out_halves = all_blocks(out_own, n)
    across_1, sent_1 = sent_back(d_two_1, d_one_1)
    sent_1, across_1, back_two = lax.optimization_barrier((sent_1, across_1, back_two))
    back_two_1 = lax.ppermute(sent_1, "seq", left_two)
    back_two = tied(back_two, (out_halves[0][2], out_halves[1][1]))
    first = finish(scal, d_own, across, back_two, dq, cosine, sine, n)
    output = place(scal, out_halves, tuple(range(n)), BF16, n)
    back_two_1 = tied(back_two_1, output)
    grad_up = scattered(tied(grad_up, back_two_1), 1)
    second = finish(scal, d_own_1, across_1, back_two_1, dq_1, cosine, sine, n)
    weights = (w_query, w_key, w_value)
    last_part = project_one_back(scal, [first, second], weights, n, n - 1, 1)
    parts = project_one_back(scal, tied([first, second], last_part), weights, n, 0, n - 1)
    parts = list(parts) + list(last_part)
    d_one_sent, d_one_kept = sum_first(parts, n)
    grad_first = outer(scal, [hidden_one], tied(first, last_part), "grad_first")
    d_one_sent, parts, grad_first = lax.optimization_barrier((d_one_sent, parts, grad_first))
    d_hidden_one = sum_second(d_one_sent, d_one_kept, n)
    d_gain_one = gain_back(scal, block_input, parts, n)
    d_hidden_one = tied(d_hidden_one, d_gain_one)
    input_grad, *input_own_halves = own_rows(
        input_kernel, scal, [own_f32, own_half, own_half], (block_input, gain_one, d_mid), d_hidden_one, "input"
    )
    input_halves = all_blocks(input_own_halves, n)
    near = (input_halves[0][2], input_halves[1][1])
    second, gains = tied((second, jnp.concatenate([d_gain_one, d_gain_two], axis=0)), near)
    grad_second = outer(scal, [hidden_one], second, "grad_second")
    gains = seq_sums(gains)
    for bit in bits_of(n):
        gains = gains + swap(gains, bit)
    early, late = tuple(range(n - 1)), (n - 1,)
    early_halves = tied([side[: n - 1] for side in input_halves], (grad_first, grad_second))
    placed = place(scal, early_halves, early, F32, n, own=input_grad)
    grad_input = place(scal, input_halves, late, F32, n, whole=placed)
    grad_first, grad_second = scattered(grad_first, 0), scattered(grad_second, 0)

    grads, after = [], input_own_halves
    for grad in (grad_down, grad_gate, grad_out):
        after = tied(grad, after)
        grads.append(after)
    after = (after, placed)
    for grad in (grad_up, grad_first):
        after = tied(grad, after)
        grads.append(after)
    grad_second = tied(grad_second, (after, grad_input))
    grad_down, grad_gate, grad_out, grad_up, grad_first = grads
    part = w_query.shape[1] // GROUPS
    grad_query, grad_key, grad_value = (
        jnp.concatenate([g[:, k * part : (k + 1) * part] for g in (grad_first, grad_second)], axis=1).astype(F32)
        for k in range(3)
    )
    return (
        output, grad_input, gains[0], grad_query, grad_key, grad_value, grad_out.astype(F32), gains[1],
        grad_gate.T.astype(F32), grad_up.T.astype(F32), grad_down.astype(F32),
    )


def solution(mesh):
    in_specs = (
        P("seq", None), P(), P(None, "tp"), P(None, "tp"), P(None, "tp"), P("tp", None), P(),
        P(None, "tp"), P(None, "tp"), P("tp", None), P("seq"), P("seq", None),
    )
    out_specs = (
        P("seq", None), P("seq", None), P("seq"), P("seq", "tp"), P("seq", "tp"), P("seq", "tp"),
        P("tp", "seq"), P("seq"), P("seq", "tp"), P("seq", "tp"), P("tp", "seq"),
    )
    return jax.shard_map(
        on_device, mesh=mesh, in_specs=in_specs, out_specs=out_specs, check_vma=False
    )
```
